256 devices in a mesh: gz: 32 (over x, y, core), gy: 8 (over z).
Axes of the slice: x: 4, y: 4, z: 8, core: 2. Of those that a mesh axis runs over, the one named last changes fastest.
Arguments:
- velocity: float32 [3, 512, 256, 512], P(None, 'gz', 'gy'), may hold values from -5 to 8
- diffusion: float32 [256, 512], P('gy'), may hold values from 0.5 to 1000
- wall_types: int32 [256, 512], P('gy'), may hold values from 0 to 3
- stretch_index: int32 [512], replicated, may hold values from 0 to 6
- bulk_target: float32 [1], replicated, may hold values from 0.5 to 1.5
Outputs:
- velocity_out: float32 [3, 512, 256, 512], P(None, 'gz', 'gy')
The draws below stay inside these ranges and needn't reach their ends.
All inputs are finite; a program needn't handle non-finite values.
Results may differ from the reference program's by a relative error of at most 0.0028.
Values sent between devices are 32-bit elements; how exact they have to be, the bound alone decides.
A program may use at most 192 MiB of HBM per device.

```python
import math
import jax
import jax.numpy as jnp
from jax import lax

NX = 512
NZ = 512
NY = 256


def draw_velocity(key, part):
    z_position = jnp.arange(NZ, dtype=jnp.float32) / NZ
    noise = jnp.clip(jax.random.normal(key, (3, NZ, NY, NX), jnp.float32), -5.0, 5.0)
    mean_part = 1.0 + 2.0 * z_position
    component_scale = jnp.array([1.0, 0.3, 0.0], jnp.float32)
    return noise + component_scale[:, None, None, None] * mean_part[None, :, None, None]


def with_ends(entries, key, least, largest):
    shape = entries.shape
    place = [jax.random.randint(jax.random.fold_in(key, axis), (), 0, shape[axis]) for axis in range(len(shape))]
    entries = entries.at[tuple(place)].set(least)
    longest = shape.index(max(shape))
    place[longest] = (place[longest] + 1) % shape[longest]
    return entries.at[tuple(place)].set(largest)


def block_scale(rng, dims, cuts, smallest, largest):
    def one(axis_at, blocks):
        steps = jax.random.uniform(jax.random.fold_in(jax.random.fold_in(rng, 6), axis_at), (blocks,), jnp.float32, smallest / len(cuts), largest / len(cuts))
        return jnp.repeat(jnp.exp(steps), dims[axis_at] // blocks).reshape((-1,) + (1,) * (len(dims) - axis_at - 1))

    gain = one(*cuts[0])
    for cut in cuts[1:]:
        gain = gain * one(*cut)
    return gain


def setup_inputs(seed: int = 0) -> dict:
    seeds = jax.random.split(jax.random.key(seed), 6)
    return {
        "velocity": draw_velocity(jax.random.fold_in(seeds[5], 71), 0),
        "diffusion": jnp.clip(jnp.exp(math.log(1000.0) - 7.6009025 * jax.random.uniform(seeds[1], (NY, NX), jnp.float32) ** block_scale(seeds[1], (NY, NX), ((0, 8),), -0.2, 0.2)), 0.5, 1000.0),
        "wall_types": with_ends(jax.random.randint(seeds[2], (NY, NX), 0, 4), jax.random.fold_in(seeds[2], 1), 0, 3).astype(jnp.int32),
        "stretch_index": with_ends(jax.random.randint(seeds[3], (NZ,), 0, 7), jax.random.fold_in(seeds[3], 1), 0, 6).astype(jnp.int32),
        "bulk_target": jnp.clip(jax.random.uniform(seeds[4], (1,), jnp.float32, 0.5, 1.5), 0.5, 1.5),
    }


def spacing(stretch_index):
    return 0.5 + 0.25 * stretch_index.astype(jnp.float32)


def face_tables(heights):
    faces = 2.0 / (heights[:-1] + heights[1:])
    padding = jnp.zeros((1,), jnp.float32)
    return jnp.concatenate([padding, faces]), jnp.concatenate([faces, padding])


def cell_rows(heights, face_left, face_right, is_first, is_last, diffusion, lower_wall, upper_wall):
    left_sum = face_left + is_first * lower_wall
    right_sum = face_right + is_last * upper_wall
    diagonal = heights + diffusion * (left_sum + right_sum)
    return -diffusion * face_left, diagonal, -diffusion * face_right


def reference(velocity, diffusion, wall_types, stretch_index, bulk_target):
    heights = spacing(stretch_index)
    face_left, face_right = face_tables(heights)
    cell_ids = jnp.arange(NZ, dtype=jnp.int32)
    is_first = (cell_ids == 0).astype(jnp.float32)
    is_last = (cell_ids == NZ - 1).astype(jnp.float32)
    lower_wall = (wall_types % 2).astype(jnp.float32) * (2.0 / heights[0])
    upper_wall = (wall_types // 2).astype(jnp.float32) * (2.0 / heights[NZ - 1])
    unit_field = jnp.ones((1, NY, NX), jnp.float32)

    def forward(carry, cell_index):
        ratio_prev, value_prev = carry
        lower_band, diagonal, upper_band = cell_rows(heights[cell_index], face_left[cell_index], face_right[cell_index], is_first[cell_index], is_last[cell_index], diffusion, lower_wall, upper_wall)
        column = lax.dynamic_index_in_dim(velocity, cell_index, axis=1, keepdims=False)
        rhs_row = jnp.concatenate([heights[cell_index] * column, heights[cell_index] * unit_field], axis=0)
        divisor = diagonal - lower_band * ratio_prev
        factor = upper_band / divisor
        solved_row = (rhs_row - lower_band[None] * value_prev) / divisor[None]
        return (factor, solved_row), (factor, solved_row)

    zero_state = (jnp.zeros((NY, NX), jnp.float32), jnp.zeros((4, NY, NX), jnp.float32))
    _, (factors, values) = lax.scan(forward, zero_state, cell_ids)

    def backward(following, row_data):
        factor, solved_row = row_data
        current = solved_row - factor[None] * following
        return current, current

    _, solved = lax.scan(backward, jnp.zeros((4, NY, NX), jnp.float32), (factors, values), reverse=True)
    flow_total = jnp.sum(heights[:, None, None] * solved[:, 0])
    weight_total = jnp.sum(heights[:, None, None] * solved[:, 3])
    volume = jnp.sum(heights) * NY * NX
    streamwise = solved[:, 0] + ((bulk_target[0] * volume - flow_total) / weight_total) * solved[:, 3]
    return jnp.stack([streamwise, solved[:, 1], solved[:, 2]], axis=0)
```

```python
import jax
import jax.numpy as jnp
from jax import lax
from jax.experimental import pallas as pl
from jax.experimental.pallas import tpu as pltpu
from jax.sharding import PartitionSpec as P

MESH = pl.DeviceIdType.MESH
F32 = jnp.float32
BLOCKS = 32
PLANES = 8
CELLS = 16
INNER = CELLS - 1
ROWS = 32
LANES = 512
TILES = LANES // 128
MSG = 24


def inverse(x):
    guess = pl.reciprocal(x, approx=True)
    return guess * (2.0 - x * guess)


def wide(tile):
    row = jnp.concatenate([tile] * TILES, axis=1)
    return jnp.concatenate([row] * (ROWS // 8), axis=0)


def across(column):
    return jnp.concatenate([column] * TILES, axis=1)


def tiles_of():
    return [(a, b) for a in range(ROWS // 8) for b in range(TILES)]


def part(x, a, b):
    return x[a * 8:(a + 1) * 8, b * 128:(b + 1) * 128]


def reduce_kernel(velocity, diffusion, walls, stretch, bulk,
                  p_ref, l_ref, r_ref, ret_ref, tbuf_ref, fix_ref,
                  v_ref, d_ref, wall_ref, stretch_ref, bulk_ref, w_ref, inv_ref, hb_ref,
                  fsend, frecv, al_ref, be_ref, dh_ref, im_ref, a_ref, g_ref, t_ref, z_ref, y_ref,
                  tsend, rsend, flow_out, flow_in, plane_out, plane_in,
                  load_sem, v_sem, send_sem, recv_sem):
    me = lax.axis_index("gz")
    plane = lax.axis_index("gy")

    def load(src, dst, sem):
        copy = pltpu.make_async_copy(src, dst, sem)
        copy.start()
        return copy

    stretch_load = load(stretch, stretch_ref, load_sem.at[0])
    bulk_load = load(bulk, bulk_ref, load_sem.at[1])
    d_load = load(diffusion, d_ref, load_sem.at[2])
    wall_load = load(walls, wall_ref, load_sem.at[3])
    v_loads = [load(velocity.at[c], v_ref.at[c], v_sem.at[c]) for c in range(3)]

    barrier = pltpu.get_barrier_semaphore()

    def greet(step, carry):
        pl.semaphore_signal(barrier, 1, device_id={"gz": lax.rem(me + step, BLOCKS)}, device_id_type=MESH)
        return carry

    def greet_plane(step, carry):
        pl.semaphore_signal(barrier, 1, device_id={"gy": lax.rem(plane + step, PLANES)}, device_id_type=MESH)
        return carry

    lax.fori_loop(1, BLOCKS, greet, 0)
    lax.fori_loop(1, PLANES, greet_plane, 0)

    stretch_load.wait()
    bulk_load.wait()

    def height(cell):
        return 0.5 + 0.25 * stretch_ref[cell].astype(F32)

    def table_row(block, carry):
        for k in range(CELLS):
            hb_ref[k, pl.ds(block, 1), :] = jnp.full((1, 128), height(block * CELLS + k), F32)
        return carry

    lax.fori_loop(0, BLOCKS, table_row, 0)

    first = me * CELLS
    h = [height(first + k) for k in range(CELLS)]
    below = height(jnp.maximum(first - 1, 0))
    above = height(jnp.minimum(first + CELLS, BLOCKS * CELLS - 1))

    def face(one, other):
        return 2.0 * inverse(jnp.full((8, 128), one + other, F32))

    ends = [below] + h
    f = [wide(face(ends[k], ends[k + 1])) for k in range(CELLS)]
    floor_scale = 2.0 * inverse(jnp.full((8, 128), height(0), F32))
    roof_scale = 2.0 * inverse(jnp.full((8, 128), height(BLOCKS * CELLS - 1), F32))
    d_load.wait()
    wall_load.wait()
    d = d_ref[...]
    lower_wall = (wall_ref[...] & 1).astype(F32) * wide(floor_scale)
    f[0] = jnp.where(me == 0, lower_wall, f[0])

    w = None
    q = d * f[0]
    for k in range(INNER):
        low, high = d * f[k], d * f[k + 1]
        pivot = h[k] + (low + high)
        if k:
            pivot = pivot - low * w
        inv = inverse(pivot)
        w = high * inv
        inv_ref[k] = inv
        w_ref[k] = w
        l_ref[k] = q * inv
        q = q * w
    left, right = l_ref[INNER - 1], w
    r_ref[INNER - 1] = right
    for k in range(INNER - 2, -1, -1):
        w = w_ref[k]
        left = l_ref[k] + w * left
        right = w * right
        l_ref[k] = left
        r_ref[k] = right

    edge_low, edge_high = d * f[0], d * f[INNER]
    total = jnp.zeros((ROWS, LANES), F32)
    for c in range(3):
        v_loads[c].wait()
        y = None
        for k in range(INNER):
            rhs = h[k] * v_ref[c, k]
            if c == 0:
                total = total + rhs
            y = rhs if k == 0 else rhs + w_ref[k - 1] * y
            p_ref[c, k] = y
        x = inv_ref[INNER - 1] * y
        p_ref[c, INNER - 1] = x
        own = h[INNER] * v_ref[c, INNER]
        if c == 0:
            total = total + own
        own = own + edge_high * x
        for k in range(INNER - 2, -1, -1):
            x = inv_ref[k] * p_ref[c, k] + w_ref[k] * x
            p_ref[c, k] = x
        other = edge_low * x
        for a, b in tiles_of():
            at = a * 8 * MSG + b
            own_row, other_row = (c * 4, 8 + c * 4) if c < 2 else (16, 20)
            fsend[pl.ds(at + own_row, 8, stride=MSG), :] = part(own, a, b)
            fsend[pl.ds(at + other_row, 8, stride=MSG), :] = part(other, a, b)
    local = jnp.zeros((8, 128), F32)
    for a, b in tiles_of():
        local = local + part(total, a, b)

    def send_all(src, dst, rows, which):
        def one(step, carry):
            peer = lax.rem(me + step, BLOCKS)
            pltpu.make_async_remote_copy(
                src_ref=src.at[pl.ds(pl.multiple_of(peer * rows, rows), rows)],
                dst_ref=dst.at[pl.ds(pl.multiple_of(me * rows, rows), rows)],
                send_sem=send_sem.at[which], recv_sem=recv_sem.at[which],
                device_id={"gz": peer}, device_id_type=MESH).start()
            return carry
        lax.fori_loop(1, BLOCKS, one, 0)
        mine = pl.ds(pl.multiple_of(me * rows, rows), rows)
        dst[mine] = src[mine]

    def wait_all(ref, rows, sem):
        span = ref.at[pl.ds(0, (BLOCKS - 1) * rows)]
        pltpu.make_async_copy(span, span, sem).wait()

    pl.semaphore_wait(barrier, BLOCKS - 1 + PLANES - 1)
    send_all(fsend, frecv, MSG, 0)

    block_id = lax.broadcasted_iota(jnp.int32, (BLOCKS, LANES), 0)
    heights = [hb_ref[k] for k in range(CELLS)]
    before = pltpu.roll(heights[INNER], 1, 0)
    after = pltpu.roll(heights[0], BLOCKS - 1, 0)
    ends = [before] + heights + [after]
    faces = [across(2.0 * inverse(ends[k] + ends[k + 1])) for k in range(CELLS + 1)]
    row_d = d_ref[pl.ds(me, 1), :]
    row_wall = wall_ref[pl.ds(me, 1), :]
    row_low = (row_wall & 1).astype(F32) * across(floor_scale[0:1])
    row_high = (row_wall >> 1).astype(F32) * across(roof_scale[0:1])
    faces[0] = jnp.where(block_id == 0, row_low, faces[0])
    faces[CELLS] = jnp.where(block_id == BLOCKS - 1, row_high, faces[CELLS])
    dd = jnp.broadcast_to(row_d, (BLOCKS, LANES))
    w = None
    q = dd * faces[0]
    first_edge = q
    alpha = None
    for k in range(INNER):
        low, high = dd * faces[k], dd * faces[k + 1]
        pivot = across(heights[k]) + (low + high)
        if k:
            pivot = pivot - low * w
        inv = inverse(pivot)
        w = high * inv
        gain = q * q * inv
        alpha = gain if alpha is None else alpha + gain
        q = q * w
    high = dd * faces[INNER]
    last_edge = dd * faces[CELLS]
    own_diagonal = across(heights[INNER]) + (high + last_edge) - high * w
    for a, b in tiles_of():
        for half in (0, 4):
            at = pl.ds(a * 64 + b + half, 8, stride=8)
            al_ref[at, :] = part(alpha, a, b)
            be_ref[at, :] = part(q, a, b)
            dh_ref[at, :] = part(own_diagonal, a, b)
    for b in range(TILES):
        for half in (0, 4):
            z_ref[pl.ds(b + half, 8, stride=8), :] = part(first_edge, 0, b)
            y_ref[pl.ds(b + half, 8, stride=8), :] = part(last_edge, BLOCKS // 8 - 1, b)
    floor_edge = z_ref[0:8]
    roof_edge = y_ref[56:64]
    zero = jnp.zeros((8, 128), F32)
    al_ref[256:264] = zero
    be_ref[256:264] = zero
    upper_half = lax.broadcasted_iota(jnp.int32, (8, 128), 0) < 4

    def rows8(at):
        return pl.ds(pl.multiple_of(at * 8, 8), 8)

    def factor(j, carry):
        g, z = carry
        beta = be_ref[rows8(j)]
        pivot = dh_ref[rows8(j)] - al_ref[rows8(j + 1)] - beta * g
        im = inverse(pivot)
        a = beta * im
        g = be_ref[rows8(j + 1)] * im
        z = a * z
        im_ref[rows8(j)] = im
        a_ref[rows8(j)] = a
        g_ref[rows8(j)] = g
        z_ref[rows8(j)] = z
        return g, z

    one = jnp.ones((8, 128), F32)
    _, z = lax.fori_loop(0, BLOCKS, factor, (zero, one))
    t = z + roof_edge * im_ref[(BLOCKS - 1) * 8:BLOCKS * 8]
    t_ref[(BLOCKS - 1) * 8:BLOCKS * 8] = t
    roof_t = t

    def unit_back(step, t):
        j = BLOCKS - 2 - step
        now = z_ref[rows8(j)] + g_ref[rows8(j)] * t
        t_ref[rows8(j)] = now
        tsend[rows8(j + 1)] = jnp.where(upper_half, now, t)
        return now

    t = lax.fori_loop(0, BLOCKS - 1, unit_back, t)
    tsend[0:8] = jnp.where(upper_half, one, t)
    send_all(tsend, tbuf_ref, 8, 1)
    height_sum = heights[0]
    for k in range(1, CELLS):
        height_sum = height_sum + heights[k]
    column = jnp.sum(height_sum, axis=0, keepdims=True)
    weight = column - (floor_edge - al_ref[0:8] - be_ref[0:8] * t) - roof_edge * (1.0 - roof_t)

    frecv[BLOCKS * MSG:(BLOCKS + 1) * MSG] = jnp.zeros((MSG, 128), F32)
    wait_all(frecv, MSG, recv_sem.at[0])

    def rowsm(j, group):
        return pl.ds(pl.multiple_of(j * MSG + group * 8, 8), 8)

    def solve_down(j, carry):
        z01, z2, flow = carry
        rho01 = frecv[rowsm(j, 0)] + frecv[rowsm(j + 1, 1)]
        rho2 = frecv[rowsm(j, 2)] + pltpu.roll(frecv[rowsm(j + 1, 2)], 4, 0)
        im, a = im_ref[rows8(j)], a_ref[rows8(j)]
        flow = flow + rho01 * t_ref[rows8(j)]
        z01 = rho01 * im + a * z01
        z2 = rho2 * im + a * z2
        z_ref[rows8(j)] = z01
        y_ref[rows8(j)] = z2
        return z01, z2, flow

    _, _, flow = lax.fori_loop(0, BLOCKS, solve_down, (zero, zero, frecv[8:16]))
    local = local + pltpu.roll(local, 4, 0)
    both = jnp.where(upper_half, local - flow, weight)
    flow_out[0:1] = jnp.sum(jnp.where(upper_half, both, 0.0), axis=0, keepdims=True)[None]
    flow_out[1:2] = jnp.sum(jnp.where(upper_half, 0.0, both), axis=0, keepdims=True)[None]

    def send_flow(step, carry):
        peer = lax.rem(me + step, BLOCKS)
        pltpu.make_async_remote_copy(
            src_ref=flow_out, dst_ref=flow_in.at[pl.ds(me * 2, 2)],
            send_sem=send_sem.at[2], recv_sem=recv_sem.at[2],
            device_id={"gz": peer}, device_id_type=MESH).start()
        return carry

    lax.fori_loop(1, BLOCKS, send_flow, 0)
    flow_in[pl.ds(me * 2, 2)] = flow_out[...]

    def solve_up(step, carry):
        s01, s2 = carry
        j = BLOCKS - 1 - step
        g = g_ref[rows8(j)]
        now01 = z_ref[rows8(j)] + g * s01
        now2 = y_ref[rows8(j)] + g * s2
        rsend[rowsm(j, 1)] = now01
        rsend[rowsm(j + 1, 0)] = now01
        rsend[rowsm(j + 1, 2)] = jnp.where(upper_half, now2, pltpu.roll(s2, 4, 0))
        return now01, now2

    _, s2 = lax.fori_loop(0, BLOCKS, solve_up, (zero, zero))
    rsend[0:8] = zero
    rsend[16:24] = jnp.where(upper_half, 0.0, pltpu.roll(s2, 4, 0))
    send_all(rsend, ret_ref, MSG, 3)

    span = flow_in.at[pl.ds(0, (BLOCKS - 1) * 2)]
    pltpu.make_async_copy(span, span, recv_sem.at[2]).wait()

    def add_up(j, carry):
        return carry[0] + flow_in[j * 2], carry[1] + flow_in[j * 2 + 1]

    line = jnp.zeros((1, 128), F32)
    flow, weight = lax.fori_loop(0, BLOCKS, add_up, (line, line))
    plane_out[0] = flow
    plane_out[1] = weight

    def send_plane(step, carry):
        peer = lax.rem(plane + step, PLANES)
        pltpu.make_async_remote_copy(
            src_ref=plane_out, dst_ref=plane_in.at[pl.ds(plane * 2, 2)],
            send_sem=send_sem.at[4], recv_sem=recv_sem.at[4],
            device_id={"gy": peer}, device_id_type=MESH).start()
        return carry

    lax.fori_loop(1, PLANES, send_plane, 0)
    plane_in[pl.ds(plane * 2, 2)] = plane_out[...]
    span = plane_in.at[pl.ds(0, (PLANES - 1) * 2)]
    pltpu.make_async_copy(span, span, recv_sem.at[4]).wait()
    flow, weight = line, line
    for j in range(PLANES):
        flow = flow + plane_in[2 * j]
        weight = weight + plane_in[2 * j + 1]
    flow = jnp.sum(jnp.broadcast_to(flow, (8, 128)), axis=1, keepdims=True)
    weight = jnp.sum(jnp.broadcast_to(weight, (8, 128)), axis=1, keepdims=True)
    lines = float(PLANES * ROWS * LANES)
    volume = jnp.broadcast_to(column, (8, 128)) * lines
    fix_ref[...] = (bulk_ref[0] * volume - jnp.broadcast_to(flow, (8, 128))) / jnp.broadcast_to(weight, (8, 128))

    wait_all(tbuf_ref, 8, recv_sem.at[1])
    wait_all(ret_ref, MSG, recv_sem.at[3])
    wait_all(fsend, MSG, send_sem.at[0])
    wait_all(tsend, 8, send_sem.at[1])
    wait_all(rsend, MSG, send_sem.at[3])
    span = flow_in.at[pl.ds(0, (BLOCKS - 1) * 2)]
    pltpu.make_async_copy(span, span, send_sem.at[2]).wait()
    span = plane_in.at[pl.ds(0, (PLANES - 1) * 2)]
    pltpu.make_async_copy(span, span, send_sem.at[4]).wait()


def finish_kernel(p_ref, l_ref, r_ref, ret_ref, tbuf_ref, fix_ref, out_hbm, out_ref, sem):
    def unpack(ref, row, step):
        bands = []
        for a in range(ROWS // 8):
            bands.append(jnp.concatenate(
                [ref[pl.ds(a * 8 * step + row + b, 8, stride=step), :] for b in range(TILES)], axis=1))
        return jnp.concatenate(bands, axis=0)

    copies = []
    for c in (1, 2, 0):
        before = unpack(ret_ref, c * 4 if c < 2 else 16, MSG)
        own = unpack(ret_ref, 8 + c * 4 if c < 2 else 20, MSG)
        fix = 0.0
        if c == 0:
            fix = wide(fix_ref[...])
            before = before - fix * unpack(tbuf_ref, 0, 8)
            own = own - fix * unpack(tbuf_ref, 4, 8)
        for k in range(CELLS):
            if k < INNER:
                value = p_ref[c, k] + l_ref[k] * before + r_ref[k] * own
            else:
                value = own
            out_ref[c, k] = value + fix if c == 0 else value
            if k % 4 == 3:
                span = pl.ds(k - 3, 4)
                copy = pltpu.make_async_copy(out_ref.at[c, span], out_hbm.at[c, span], sem.at[c, k // 4])
                copy.start()
                copies.append(copy)
    for copy in copies:
        copy.wait()


def shards(velocity, diffusion, wall_types, stretch_index, bulk_target):
    hbm = pl.BlockSpec(memory_space=pltpu.HBM)
    vmem = pl.BlockSpec(memory_space=pltpu.VMEM)
    plane = (ROWS, LANES)
    mids = pl.pallas_call(
        reduce_kernel,
        name="reduce_and_solve",
        out_shape=[
            pltpu.VMEM((3, INNER) + plane, F32),
            pltpu.VMEM((INNER,) + plane, F32),
            pltpu.VMEM((INNER,) + plane, F32),
            pltpu.VMEM((BLOCKS * MSG, 128), F32),
            pltpu.VMEM((BLOCKS * 8, 128), F32),
            pltpu.VMEM((8, 128), F32),
        ],
        in_specs=[hbm] * 5,
        out_specs=[vmem] * 6,
        scratch_shapes=[
            pltpu.VMEM((3, CELLS) + plane, F32),
            pltpu.VMEM(plane, F32),
            pltpu.VMEM(plane, jnp.int32),
            pltpu.SMEM((BLOCKS * CELLS,), jnp.int32),
            pltpu.SMEM((1,), F32),
            pltpu.VMEM((INNER,) + plane, F32),
            pltpu.VMEM((INNER,) + plane, F32),
            pltpu.VMEM((CELLS, BLOCKS, 128), F32),
            pltpu.VMEM((BLOCKS * MSG, 128), F32),
            pltpu.VMEM(((BLOCKS + 1) * MSG, 128), F32),
            *[pltpu.VMEM(((BLOCKS + 1) * 8, 128), F32)] * 9,
            pltpu.VMEM((BLOCKS * 8, 128), F32),
            pltpu.VMEM(((BLOCKS + 1) * MSG, 128), F32),
            pltpu.VMEM((2, 1, 128), F32),
            pltpu.VMEM((BLOCKS * 2, 1, 128), F32),
            pltpu.VMEM((2, 1, 128), F32),
            pltpu.VMEM((PLANES * 2, 1, 128), F32),
            pltpu.SemaphoreType.DMA((4,)),
            pltpu.SemaphoreType.DMA((3,)),
            pltpu.SemaphoreType.DMA((5,)),
            pltpu.SemaphoreType.DMA((5,)),
        ],
        compiler_params=pltpu.CompilerParams(
            collective_id=0, has_side_effects=True, vmem_limit_bytes=24 * 2**20),
    )(*[pltpu.with_memory_space_constraint(x, pltpu.HBM)
        for x in (velocity, diffusion, wall_types, stretch_index)], bulk_target)
    return pl.pallas_call(
        finish_kernel,
        name="finish",
        out_shape=jax.ShapeDtypeStruct((3, CELLS) + plane, F32),
        in_specs=[vmem] * 6,
        out_specs=hbm,
        scratch_shapes=[pltpu.VMEM((3, CELLS) + plane, F32), pltpu.SemaphoreType.DMA((3, 4))],
        compiler_params=pltpu.CompilerParams(vmem_limit_bytes=24 * 2**20),
    )(*mids)


def solution(mesh):
    return jax.shard_map(
        shards,
        mesh=mesh,
        in_specs=(P(None, "gz", "gy", None), P("gy", None), P("gy", None), P(), P()),
        out_specs=P(None, "gz", "gy", None),
        check_vma=False,
    )
```

```python
import jax
import jax.numpy as jnp
from jax import lax
from jax.experimental import pallas as pl
from jax.experimental.pallas import tpu as pltpu
from jax.sharding import PartitionSpec as P

MESH = pl.DeviceIdType.MESH
F32 = jnp.float32
BLOCKS = 32
PLANES = 8
CELLS = 16
INNER = CELLS - 1
ROWS = 32
LANES = 512
TILES = LANES // 128
MSG = 8
GROUP = 8


def inverse(x):
    guess = pl.reciprocal(x, approx=True)
    return guess * (2.0 - x * guess)


def wide(tile):
    row = jnp.concatenate([tile] * TILES, axis=1)
    return jnp.concatenate([row] * (ROWS // 8), axis=0)


def across(column):
    return jnp.concatenate([column] * TILES, axis=1)


def tiles_of():
    return [(a, b) for a in range(ROWS // 8) for b in range(TILES)]


def part(x, a, b):
    return x[a * 8:(a + 1) * 8, b * 128:(b + 1) * 128]


def reduce_kernel(velocity, diffusion, walls, stretch, bulk,
                  p_ref, l_ref, r_ref, ret_ref, tbuf_ref, fix_ref,
                  v_ref, d_ref, wall_ref, stretch_ref, bulk_ref, w_ref, inv_ref, hb_ref,
                  fsend, frecv, al_ref, be_ref, dh_ref, im_ref, a_ref, g_ref, t_ref, z_ref, y_ref,
                  tsend, rsend, flow_out, flow_in, plane_out, plane_in,
                  load_sem, v_sem, send_sem, recv_sem):
    me = lax.axis_index("gz")
    plane = lax.axis_index("gy")

    def load(src, dst, sem):
        copy = pltpu.make_async_copy(src, dst, sem)
        copy.start()
        return copy

    stretch_load = load(stretch, stretch_ref, load_sem.at[0])
    d_load = load(diffusion, d_ref, load_sem.at[2])
    wall_load = load(walls, wall_ref, load_sem.at[3])
    v_loads = [load(velocity.at[c], v_ref.at[c], v_sem.at[c]) for c in range(3)]
    bulk_load = load(bulk, bulk_ref, load_sem.at[1])

    barrier = pltpu.get_barrier_semaphore()

    def greet(step, carry):
        pl.semaphore_signal(barrier, 1, device_id={"gz": lax.rem(me + step, BLOCKS)}, device_id_type=MESH)
        return carry

    def greet_plane(step, carry):
        pl.semaphore_signal(barrier, 1, device_id={"gy": lax.rem(plane + step, PLANES)}, device_id_type=MESH)
        return carry

    lax.fori_loop(1, BLOCKS, greet, 0)
    lax.fori_loop(1, PLANES, greet_plane, 0)

    stretch_load.wait()

    def height(cell):
        return 0.5 + 0.25 * stretch_ref[cell].astype(F32)

    first = me * CELLS
    h = [height(first + k) for k in range(CELLS)]
    below = height(jnp.maximum(first - 1, 0))

    def face(one, other):
        return 2.0 * inverse(jnp.full((8, 128), one + other, F32))

    ends = [below] + h
    f = [wide(face(ends[k], ends[k + 1])) for k in range(CELLS)]
    floor_scale = 2.0 * inverse(jnp.full((8, 128), height(0), F32))
    roof_scale = 2.0 * inverse(jnp.full((8, 128), height(BLOCKS * CELLS - 1), F32))
    d_load.wait()
    wall_load.wait()
    d = d_ref[...]
    lower_wall = (wall_ref[...] & 1).astype(F32) * wide(floor_scale)
    edge_low = d * jnp.where(me == 0, lower_wall, f[0])

    w = None
    low = edge_low
    for k in range(INNER):
        high = d * f[k + 1]
        pivot = h[k] + (low + high)
        if k:
            pivot = pivot - low * w
        inv = inverse(pivot)
        w = high * inv
        low = high
        inv_ref[k] = inv
        w_ref[k] = w
    edge_high = low

    def send_all(src, dst, which):
        x, y, core = me // 8, lax.rem(me // 2, 4), lax.rem(me, 2)

        def offset(place):
            return jnp.where(place == 0, 2, jnp.where(place == 1, 1, jnp.where(place == 2, 3, 0)))

        def one(step, carry):
            to_x = lax.rem(x + offset(step // 8), 4)
            to_y = lax.rem(y + offset(lax.rem(step // 2, 4)), 4)
            to_core = lax.rem(core + 1 + lax.rem(step, 2), 2)
            peer = to_x * 8 + to_y * 2 + to_core
            pltpu.make_async_remote_copy(
                src_ref=src.at[pl.ds(pl.multiple_of(peer * MSG, MSG), MSG)],
                dst_ref=dst.at[pl.ds(pl.multiple_of(me * MSG, MSG), MSG)],
                send_sem=send_sem.at[which], recv_sem=recv_sem.at[which],
                device_id={"gz": peer}, device_id_type=MESH).start()
            return carry

        lax.fori_loop(0, BLOCKS - 1, one, 0)
        mine = pl.ds(pl.multiple_of(me * MSG, MSG), MSG)
        dst[mine] = src[mine]

    def wait_all(ref, rows, sem):
        span = ref.at[pl.ds(0, (BLOCKS - 1) * rows)]
        pltpu.make_async_copy(span, span, sem).wait()

    total = jnp.zeros((ROWS, LANES), F32)
    for c in range(3):
        v_loads[c].wait()
        y = None
        for k in range(INNER):
            rhs = h[k] * v_ref[c, k]
            if c == 0:
                total = total + rhs
            y = rhs if k == 0 else rhs + w_ref[k - 1] * y
            p_ref[c, k] = y
        x = inv_ref[INNER - 1] * y
        p_ref[c, INNER - 1] = x
        own = h[INNER] * v_ref[c, INNER]
        if c == 0:
            total = total + own
        own = own + edge_high * x
        for k in range(INNER - 2, -1, -1):
            x = inv_ref[k] * p_ref[c, k] + w_ref[k] * x
            p_ref[c, k] = x
        other = edge_low * x
        for a, b in tiles_of():
            at = a * 8 * MSG + b
            fsend[c, pl.ds(at, 8, stride=MSG), :] = part(own, a, b)
            fsend[c, pl.ds(at + 4, 8, stride=MSG), :] = part(other, a, b)
        if c == 0:
            pl.semaphore_wait(barrier, BLOCKS - 1 + PLANES - 1)
        send_all(fsend.at[c], frecv.at[c], c)
    local = jnp.zeros((8, 128), F32)
    for a, b in tiles_of():
        local = local + part(total, a, b)

    def table_row(block, carry):
        for k in range(CELLS):
            hb_ref[k, pl.ds(block, 1), :] = jnp.full((1, 128), height(block * CELLS + k), F32)
        return carry

    lax.fori_loop(0, BLOCKS, table_row, 0)
    block_id = lax.broadcasted_iota(jnp.int32, (BLOCKS, LANES), 0)
    heights = [hb_ref[k] for k in range(CELLS)]
    before = pltpu.roll(heights[INNER], 1, 0)
    after = pltpu.roll(heights[0], BLOCKS - 1, 0)
    ends = [before] + heights + [after]
    faces = [across(2.0 * inverse(ends[k] + ends[k + 1])) for k in range(CELLS + 1)]
    row_d = d_ref[pl.ds(me, 1), :]
    row_wall = wall_ref[pl.ds(me, 1), :]
    row_low = (row_wall & 1).astype(F32) * across(floor_scale[0:1])
    row_high = (row_wall >> 1).astype(F32) * across(roof_scale[0:1])
    faces[0] = jnp.where(block_id == 0, row_low, faces[0])
    faces[CELLS] = jnp.where(block_id == BLOCKS - 1, row_high, faces[CELLS])
    dd = jnp.broadcast_to(row_d, (BLOCKS, LANES))
    w = None
    q = dd * faces[0]
    first_edge = q
    alpha = None
    for k in range(INNER):
        low, high = dd * faces[k], dd * faces[k + 1]
        pivot = across(heights[k]) + (low + high)
        if k:
            pivot = pivot - low * w
        inv = inverse(pivot)
        w = high * inv
        gain = q * q * inv
        alpha = gain if alpha is None else alpha + gain
        q = q * w
    high = dd * faces[INNER]
    last_edge = dd * faces[CELLS]
    own_diagonal = across(heights[INNER]) + (high + last_edge) - high * w
    for a, b in tiles_of():
        for half in (0, 4):
            at = pl.ds(a * 64 + b + half, 8, stride=8)
            al_ref[at, :] = part(alpha, a, b)
            be_ref[at, :] = part(q, a, b)
            dh_ref[at, :] = part(own_diagonal, a, b)
    for b in range(TILES):
        for half in (0, 4):
            z_ref[pl.ds(b + half, 8, stride=8), :] = part(first_edge, 0, b)
            y_ref[pl.ds(b + half, 8, stride=8), :] = part(last_edge, BLOCKS // 8 - 1, b)
    floor_edge = z_ref[0:8]
    roof_edge = y_ref[56:64]
    zero = jnp.zeros((8, 128), F32)
    one = jnp.ones((8, 128), F32)
    al_ref[256:264] = zero
    be_ref[256:264] = zero
    upper_half = lax.broadcasted_iota(jnp.int32, (8, 128), 0) < 4

    def rows8(at):
        return pl.ds(pl.multiple_of(at * 8, 8), 8)

    def sweep(step, carry, backward=False):
        def group(at, carry):
            for u in range(GROUP):
                j = at * GROUP + u
                carry = step(BLOCKS - 1 - j if backward else j, carry)
            return carry
        return lax.fori_loop(0, BLOCKS // GROUP, group, carry)

    def factor(j, carry):
        g, z = carry
        beta = be_ref[rows8(j)]
        pivot = dh_ref[rows8(j)] - al_ref[rows8(j + 1)] - beta * g
        im = inverse(pivot)
        a = beta * im
        g = be_ref[rows8(j + 1)] * im
        z = a * z
        im_ref[rows8(j)] = im
        a_ref[rows8(j)] = a
        g_ref[rows8(j)] = g
        z_ref[rows8(j)] = z
        return g, z

    sweep(factor, (zero, one))
    last = pl.ds((BLOCKS - 1) * 8, 8)
    z_ref[last] = z_ref[last] + roof_edge * im_ref[last]

    def unit_back(j, t):
        now = z_ref[rows8(j)] + g_ref[rows8(j)] * t
        t_ref[rows8(j)] = now
        tsend[rows8(j + 1)] = jnp.where(upper_half, now, t)
        return now

    t = sweep(unit_back, zero, backward=True)
    tsend[0:8] = jnp.where(upper_half, one, t)
    send_all(tsend, tbuf_ref, 6)
    height_sum = heights[0]
    for k in range(1, CELLS):
        height_sum = height_sum + heights[k]
    column = jnp.sum(height_sum, axis=0, keepdims=True)
    weight = column - (floor_edge - al_ref[0:8] - be_ref[0:8] * t) - roof_edge * (1.0 - t_ref[last])

    left = edge_low
    for k in range(INNER):
        l_ref[k] = left * inv_ref[k]
        left = left * w_ref[k]
    left, right = l_ref[INNER - 1], w_ref[INNER - 1]
    r_ref[INNER - 1] = right
    for k in range(INNER - 2, -1, -1):
        w = w_ref[k]
        left = l_ref[k] + w * left
        right = w * right
        l_ref[k] = left
        r_ref[k] = right

    def solve(c):
        frecv[c, pl.ds(BLOCKS * MSG, MSG)] = zero
        wait_all(frecv.at[c], MSG, recv_sem.at[c])

        def down(j, carry):
            z, flow = carry
            rho = frecv[c, rows8(j)] + pltpu.roll(frecv[c, rows8(j + 1)], 4, 0)
            if c == 0:
                flow = flow + rho * t_ref[rows8(j)]
            z = rho * im_ref[rows8(j)] + a_ref[rows8(j)] * z
            z_ref[rows8(j)] = z
            return z, flow

        _, flow = sweep(down, (zero, pltpu.roll(frecv[c, 0:8], 4, 0)))
        if c == 0:
            sums = local + pltpu.roll(local, 4, 0)
            flow_out[0] = jnp.sum(jnp.where(upper_half, sums - flow, 0.0), axis=0, keepdims=True)
            flow_out[1] = jnp.sum(jnp.where(upper_half, weight, 0.0), axis=0, keepdims=True)

            def send_flow(step, carry):
                pltpu.make_async_remote_copy(
                    src_ref=flow_out, dst_ref=flow_in.at[pl.ds(me * 2, 2)],
                    send_sem=send_sem.at[7], recv_sem=recv_sem.at[7],
                    device_id={"gz": lax.rem(me + step, BLOCKS)}, device_id_type=MESH).start()
                return carry

            lax.fori_loop(1, BLOCKS, send_flow, 0)
            flow_in[pl.ds(me * 2, 2)] = flow_out[...]

        def up(j, s):
            now = z_ref[rows8(j)] + g_ref[rows8(j)] * s
            rsend[c, rows8(j + 1)] = jnp.where(upper_half, now, pltpu.roll(s, 4, 0))
            return now

        s = sweep(up, zero, backward=True)
        rsend[c, 0:8] = jnp.where(upper_half, 0.0, pltpu.roll(s, 4, 0))
        send_all(rsend.at[c], ret_ref.at[c], 3 + c)

    for c in range(3):
        solve(c)

    wait_all(flow_in, 2, recv_sem.at[7])

    def add_up(j, carry):
        return carry[0] + flow_in[j * 2], carry[1] + flow_in[j * 2 + 1]

    line = jnp.zeros((1, 128), F32)
    flow, weight = lax.fori_loop(0, BLOCKS, add_up, (line, line))
    plane_out[0] = flow
    plane_out[1] = weight

    def send_plane(step, carry):
        peer = lax.rem(plane + step, PLANES)
        pltpu.make_async_remote_copy(
            src_ref=plane_out, dst_ref=plane_in.at[pl.ds(plane * 2, 2)],
            send_sem=send_sem.at[8], recv_sem=recv_sem.at[8],
            device_id={"gy": peer}, device_id_type=MESH).start()
        return carry

    lax.fori_loop(1, PLANES, send_plane, 0)
    plane_in[pl.ds(plane * 2, 2)] = plane_out[...]

    wait_all(ret_ref.at[1], MSG, recv_sem.at[4])
    before, own = unpack(ret_ref.at[1], 0), unpack(ret_ref.at[1], 4)
    for k in range(INNER):
        p_ref[1, k] = p_ref[1, k] + l_ref[k] * before + r_ref[k] * own
    p_ref[1, INNER] = own

    bulk_load.wait()
    span = plane_in.at[pl.ds(0, (PLANES - 1) * 2)]
    pltpu.make_async_copy(span, span, recv_sem.at[8]).wait()
    flow, weight = line, line
    for j in range(PLANES):
        flow = flow + plane_in[2 * j]
        weight = weight + plane_in[2 * j + 1]
    flow = jnp.sum(jnp.broadcast_to(flow, (8, 128)), axis=1, keepdims=True)
    weight = jnp.sum(jnp.broadcast_to(weight, (8, 128)), axis=1, keepdims=True)
    lines = float(PLANES * ROWS * LANES)
    volume = jnp.broadcast_to(column, (8, 128)) * lines
    fix_ref[...] = (bulk_ref[0] * volume - jnp.broadcast_to(flow, (8, 128))) / jnp.broadcast_to(weight, (8, 128))

    for c in range(3):
        wait_all(fsend.at[c], MSG, send_sem.at[c])
        wait_all(rsend.at[c], MSG, send_sem.at[3 + c])
    wait_all(tsend, MSG, send_sem.at[6])
    wait_all(flow_in, 2, send_sem.at[7])
    span = plane_in.at[pl.ds(0, (PLANES - 1) * 2)]
    pltpu.make_async_copy(span, span, send_sem.at[8]).wait()
    wait_all(tbuf_ref, MSG, recv_sem.at[6])
    wait_all(ret_ref.at[0], MSG, recv_sem.at[3])
    wait_all(ret_ref.at[2], MSG, recv_sem.at[5])


def unpack(ref, row):
    bands = []
    for a in range(ROWS // 8):
        bands.append(jnp.concatenate(
            [ref[pl.ds(a * 8 * MSG + row + b, 8, stride=MSG), :] for b in range(TILES)], axis=1))
    return jnp.concatenate(bands, axis=0)


def finish_kernel(p_ref, l_ref, r_ref, ret_ref, tbuf_ref, fix_ref, out_hbm, out_ref, sem):
    copies = []

    def write(src, c, start, count):
        copy = pltpu.make_async_copy(
            src.at[c, pl.ds(start, count)], out_hbm.at[c, pl.ds(start, count)], sem.at[c, start // 4])
        copy.start()
        copies.append(copy)

    for start in range(0, CELLS, 4):
        write(p_ref, 1, start, 4)
    for c in (2, 0):
        before, own = unpack(ret_ref.at[c], 0), unpack(ret_ref.at[c], 4)
        if c == 0:
            fix = wide(fix_ref[...])
            before = before - fix * unpack(tbuf_ref, 0)
            own = own - fix * unpack(tbuf_ref, 4)
        for k in range(CELLS):
            if k < INNER:
                value = p_ref[c, k] + l_ref[k] * before + r_ref[k] * own
            else:
                value = own
            out_ref[c, k] = value + fix if c == 0 else value
            if k % 4 == 3:
                write(out_ref, c, k - 3, 4)
    for copy in copies:
        copy.wait()


def shards(velocity, diffusion, wall_types, stretch_index, bulk_target):
    hbm = pl.BlockSpec(memory_space=pltpu.HBM)
    vmem = pl.BlockSpec(memory_space=pltpu.VMEM)
    plane = (ROWS, LANES)
    mids = pl.pallas_call(
        reduce_kernel,
        name="reduce_and_solve",
        out_shape=[
            pltpu.VMEM((3, CELLS) + plane, F32),
            pltpu.VMEM((INNER,) + plane, F32),
            pltpu.VMEM((INNER,) + plane, F32),
            pltpu.VMEM((3, BLOCKS * MSG, 128), F32),
            pltpu.VMEM((BLOCKS * MSG, 128), F32),
            pltpu.VMEM((8, 128), F32),
        ],
        in_specs=[hbm] * 5,
        out_specs=[vmem] * 6,
        scratch_shapes=[
            pltpu.VMEM((3, CELLS) + plane, F32),
            pltpu.VMEM(plane, F32),
            pltpu.VMEM(plane, jnp.int32),
            pltpu.SMEM((BLOCKS * CELLS,), jnp.int32),
            pltpu.SMEM((1,), F32),
            pltpu.VMEM((INNER,) + plane, F32),
            pltpu.VMEM((INNER,) + plane, F32),
            pltpu.VMEM((CELLS, BLOCKS, 128), F32),
            pltpu.VMEM((3, BLOCKS * MSG, 128), F32),
            pltpu.VMEM((3, (BLOCKS + 1) * MSG, 128), F32),
            *[pltpu.VMEM(((BLOCKS + 1) * 8, 128), F32)] * 9,
            pltpu.VMEM(((BLOCKS + 1) * MSG, 128), F32),
            pltpu.VMEM((3, (BLOCKS + 1) * MSG, 128), F32),
            pltpu.VMEM((2, 1, 128), F32),
            pltpu.VMEM((BLOCKS * 2, 1, 128), F32),
            pltpu.VMEM((2, 1, 128), F32),
            pltpu.VMEM((PLANES * 2, 1, 128), F32),
            pltpu.SemaphoreType.DMA((4,)),
            pltpu.SemaphoreType.DMA((3,)),
            pltpu.SemaphoreType.DMA((9,)),
            pltpu.SemaphoreType.DMA((9,)),
        ],
        compiler_params=pltpu.CompilerParams(
            collective_id=0, has_side_effects=True, vmem_limit_bytes=24 * 2**20),
    )(*[pltpu.with_memory_space_constraint(x, pltpu.HBM)
        for x in (velocity, diffusion, wall_types, stretch_index)], bulk_target)
    return pl.pallas_call(
        finish_kernel,
        name="finish",
        out_shape=jax.ShapeDtypeStruct((3, CELLS) + plane, F32),
        in_specs=[vmem] * 6,
        out_specs=hbm,
        scratch_shapes=[pltpu.VMEM((3, CELLS) + plane, F32), pltpu.SemaphoreType.DMA((3, 4))],
        compiler_params=pltpu.CompilerParams(vmem_limit_bytes=24 * 2**20),
    )(*mids)


def solution(mesh):
    return jax.shard_map(
        shards,
        mesh=mesh,
        in_specs=(P(None, "gz", "gy", None), P("gy", None), P("gy", None), P(), P()),
        out_specs=P(None, "gz", "gy", None),
        check_vma=False,
    )
```

```python
import jax
import jax.numpy as jnp
from jax import lax
from jax.experimental import pallas as pl
from jax.experimental.pallas import tpu as pltpu
from jax.sharding import PartitionSpec as P

MESH = pl.DeviceIdType.MESH
F32 = jnp.float32
BLOCKS = 32
PLANES = 8
CELLS = 16
INNER = CELLS - 1
ROWS = 32
LANES = 512
TILES = LANES // 128
MSG = 8
GROUP = 8


FAR_FIRST = sorted(range(1, BLOCKS), key=lambda i: -min(i // 8, 4 - i // 8) - min(i // 2 % 4, 4 - i // 2 % 4))


def inverse(x):
    guess = pl.reciprocal(x, approx=True)
    return guess * (2.0 - x * guess)


def wide(tile):
    row = jnp.concatenate([tile] * TILES, axis=1)
    return jnp.concatenate([row] * (ROWS // 8), axis=0)


def across(column):
    return jnp.concatenate([column] * TILES, axis=1)


def tiles_of():
    return [(a, b) for a in range(ROWS // 8) for b in range(TILES)]


def part(x, a, b):
    return x[a * 8:(a + 1) * 8, b * 128:(b + 1) * 128]


def reduce_kernel(velocity, diffusion, walls, stretch, bulk,
                  p_ref, u_ref, fix_ref,
                  l_ref, r_ref, ret_ref, tbuf_ref, v_ref, d_ref, wall_ref, stretch_ref, bulk_ref, w_ref, inv_ref, hb_ref,
                  fsend, frecv, al_ref, be_ref, dh_ref, im_ref, a_ref, g_ref, t_ref, z_ref, y_ref,
                  tsend, rsend, flow_out, flow_in, plane_out, plane_in,
                  load_sem, v_sem, send_sem, recv_sem, plane_sem):
    me = lax.axis_index("gz")
    plane = lax.axis_index("gy")

    def load(src, dst, sem):
        copy = pltpu.make_async_copy(src, dst, sem)
        copy.start()
        return copy

    barrier = pltpu.get_barrier_semaphore()

    def greet(step, carry):
        pl.semaphore_signal(barrier, 1, device_id={"gz": lax.rem(me + step, BLOCKS)}, device_id_type=MESH)
        return carry

    def greet_plane(other, carry):
        pl.semaphore_signal(barrier, 1, device_id={"gy": other}, device_id_type=MESH)
        return carry

    lax.fori_loop(1, BLOCKS, greet, 0)
    lax.fori_loop(plane + 1, PLANES, greet_plane, 0)

    stretch_load = load(stretch, stretch_ref, load_sem.at[0])
    d_load = load(diffusion, d_ref, load_sem.at[2])
    wall_load = load(walls, wall_ref, load_sem.at[3])
    v_loads = [load(velocity.at[0], v_ref.at[0], v_sem.at[0])]

    stretch_load.wait()

    def height(cell):
        return 0.5 + 0.25 * stretch_ref[cell].astype(F32)

    first = me * CELLS
    h = [height(first + k) for k in range(CELLS)]
    below = height(jnp.maximum(first - 1, 0))

    def face(one, other):
        return 2.0 * inverse(jnp.full((8, 128), one + other, F32))

    ends = [below] + h
    f = [wide(face(ends[k], ends[k + 1])) for k in range(CELLS)]
    floor_scale = 2.0 * inverse(jnp.full((8, 128), height(0), F32))
    roof_scale = 2.0 * inverse(jnp.full((8, 128), height(BLOCKS * CELLS - 1), F32))
    d_load.wait()
    wall_load.wait()
    v_loads += [load(velocity.at[c], v_ref.at[c], v_sem.at[c]) for c in (1, 2)]
    bulk_load = load(bulk, bulk_ref, load_sem.at[1])
    d = d_ref[...]
    lower_wall = (wall_ref[...] & 1).astype(F32) * wide(floor_scale)
    edge_low = d * jnp.where(me == 0, lower_wall, f[0])

    w = None
    low = edge_low
    for k in range(INNER):
        high = d * f[k + 1]
        pivot = h[k] + (low + high)
        if k:
            pivot = pivot - low * w
        inv = inverse(pivot)
        w = high * inv
        low = high
        inv_ref[k] = inv
        w_ref[k] = w
    edge_high = low

    def send_all(src, dst, which):
        x, y, core = me // 8, lax.rem(me // 2, 4), lax.rem(me, 2)

        for step in FAR_FIRST:
            peer = lax.rem(x + step // 8, 4) * 8 + lax.rem(y + (step // 2) % 4, 4) * 2 + (lax.rem(core + step % 2, 2))
            pltpu.make_async_remote_copy(
                src_ref=src.at[pl.ds(pl.multiple_of(peer * MSG, MSG), MSG)],
                dst_ref=dst.at[pl.ds(pl.multiple_of(me * MSG, MSG), MSG)],
                send_sem=send_sem.at[which], recv_sem=recv_sem.at[which],
                device_id={"gz": peer}, device_id_type=MESH).start()
        mine = pl.ds(pl.multiple_of(me * MSG, MSG), MSG)
        dst[mine] = src[mine]

    def wait_all(ref, rows, sem):
        span = ref.at[pl.ds(0, (BLOCKS - 1) * rows)]
        pltpu.make_async_copy(span, span, sem).wait()

    def answer_plane(other, carry):
        pl.semaphore_signal(plane_sem, 1, device_id={"gy": other}, device_id_type=MESH)
        return carry

    total = jnp.zeros((ROWS, LANES), F32)
    for c in range(3):
        v_loads[c].wait()
        y = None
        for k in range(INNER):
            rhs = h[k] * v_ref[c, k]
            if c == 0:
                total = total + rhs
            y = rhs if k == 0 else rhs + w_ref[k - 1] * y
            p_ref[c, k] = y
        x = inv_ref[INNER - 1] * y
        p_ref[c, INNER - 1] = x
        own = h[INNER] * v_ref[c, INNER]
        if c == 0:
            total = total + own
        own = own + edge_high * x
        for k in range(INNER - 2, -1, -1):
            x = inv_ref[k] * p_ref[c, k] + w_ref[k] * x
            p_ref[c, k] = x
        other = edge_low * x
        for a, b in tiles_of():
            at = a * 8 * MSG + b
            fsend[c, pl.ds(at, 8, stride=MSG), :] = part(own, a, b)
            fsend[c, pl.ds(at + 4, 8, stride=MSG), :] = part(other, a, b)
        if c == 0:
            pl.semaphore_wait(barrier, BLOCKS - 1 + plane)
        send_all(fsend.at[c], frecv.at[c], c)
        if c == 0:
            lax.fori_loop(0, plane, answer_plane, 0)
    local = jnp.zeros((8, 128), F32)
    for a, b in tiles_of():
        local = local + part(total, a, b)

    def table_row(block, carry):
        for k in range(CELLS):
            hb_ref[k, pl.ds(block, 1), :] = jnp.full((1, 128), height(block * CELLS + k), F32)
        return carry

    lax.fori_loop(0, BLOCKS, table_row, 0)
    block_id = lax.broadcasted_iota(jnp.int32, (BLOCKS, LANES), 0)
    heights = [hb_ref[k] for k in range(CELLS)]
    before = pltpu.roll(heights[INNER], 1, 0)
    after = pltpu.roll(heights[0], BLOCKS - 1, 0)
    ends = [before] + heights + [after]
    faces = [across(2.0 * inverse(ends[k] + ends[k + 1])) for k in range(CELLS + 1)]
    row_d = d_ref[pl.ds(me, 1), :]
    row_wall = wall_ref[pl.ds(me, 1), :]
    row_low = (row_wall & 1).astype(F32) * across(floor_scale[0:1])
    row_high = (row_wall >> 1).astype(F32) * across(roof_scale[0:1])
    faces[0] = jnp.where(block_id == 0, row_low, faces[0])
    faces[CELLS] = jnp.where(block_id == BLOCKS - 1, row_high, faces[CELLS])
    dd = jnp.broadcast_to(row_d, (BLOCKS, LANES))
    w = None
    q = dd * faces[0]
    first_edge = q
    alpha = None
    for k in range(INNER):
        low, high = dd * faces[k], dd * faces[k + 1]
        pivot = across(heights[k]) + (low + high)
        if k:
            pivot = pivot - low * w
        inv = inverse(pivot)
        w = high * inv
        gain = q * q * inv
        alpha = gain if alpha is None else alpha + gain
        q = q * w
    high = dd * faces[INNER]
    last_edge = dd * faces[CELLS]
    own_diagonal = across(heights[INNER]) + (high + last_edge) - high * w
    for a, b in tiles_of():
        for half in (0, 4):
            at = pl.ds(a * 64 + b + half, 8, stride=8)
            al_ref[at, :] = part(alpha, a, b)
            be_ref[at, :] = part(q, a, b)
            dh_ref[at, :] = part(own_diagonal, a, b)
    for b in range(TILES):
        for half in (0, 4):
            z_ref[pl.ds(b + half, 8, stride=8), :] = part(first_edge, 0, b)
            y_ref[pl.ds(b + half, 8, stride=8), :] = part(last_edge, BLOCKS // 8 - 1, b)
    floor_edge = z_ref[0:8]
    roof_edge = y_ref[56:64]
    zero = jnp.zeros((8, 128), F32)
    one = jnp.ones((8, 128), F32)
    al_ref[256:264] = zero
    be_ref[256:264] = zero
    upper_half = lax.broadcasted_iota(jnp.int32, (8, 128), 0) < 4

    def rows8(at):
        return pl.ds(pl.multiple_of(at * 8, 8), 8)

    def sweep(step, carry, backward=False):
        def group(at, carry):
            for u in range(GROUP):
                j = at * GROUP + u
                carry = step(BLOCKS - 1 - j if backward else j, carry)
            return carry
        return lax.fori_loop(0, BLOCKS // GROUP, group, carry)

    def factor(j, carry):
        g, z = carry
        beta = be_ref[rows8(j)]
        pivot = dh_ref[rows8(j)] - al_ref[rows8(j + 1)] - beta * g
        im = inverse(pivot)
        a = beta * im
        g = be_ref[rows8(j + 1)] * im
        z = a * z
        im_ref[rows8(j)] = im
        a_ref[rows8(j)] = a
        g_ref[rows8(j)] = g
        z_ref[rows8(j)] = z
        return g, z

    sweep(factor, (zero, one))
    last = pl.ds((BLOCKS - 1) * 8, 8)
    z_ref[last] = z_ref[last] + roof_edge * im_ref[last]

    def unit_back(j, t):
        now = z_ref[rows8(j)] + g_ref[rows8(j)] * t
        t_ref[rows8(j)] = now
        tsend[rows8(j + 1)] = jnp.where(upper_half, now, t)
        return now

    t = sweep(unit_back, zero, backward=True)
    tsend[0:8] = jnp.where(upper_half, one, t)
    height_sum = heights[0]
    for k in range(1, CELLS):
        height_sum = height_sum + heights[k]
    column = jnp.sum(height_sum, axis=0, keepdims=True)
    weight = column - (floor_edge - al_ref[0:8] - be_ref[0:8] * t) - roof_edge * (1.0 - t_ref[last])

    def solve(c):
        frecv[c, pl.ds(BLOCKS * MSG, MSG)] = zero
        wait_all(frecv.at[c], MSG, recv_sem.at[c])

        def down(j, carry):
            z, flow = carry
            rho = frecv[c, rows8(j)] + pltpu.roll(frecv[c, rows8(j + 1)], 4, 0)
            if c == 0:
                flow = flow + rho * t_ref[rows8(j)]
            z = rho * im_ref[rows8(j)] + a_ref[rows8(j)] * z
            z_ref[rows8(j)] = z
            return z, flow

        _, flow = sweep(down, (zero, pltpu.roll(frecv[c, 0:8], 4, 0)))
        if c == 0:
            sums = local + pltpu.roll(local, 4, 0)
            flow_out[0] = jnp.sum(jnp.where(upper_half, sums - flow, 0.0), axis=0, keepdims=True)
            flow_out[1] = jnp.sum(jnp.where(upper_half, weight, 0.0), axis=0, keepdims=True)

            def send_flow(step, carry):
                pltpu.make_async_remote_copy(
                    src_ref=flow_out, dst_ref=flow_in.at[pl.ds(me * 2, 2)],
                    send_sem=send_sem.at[7], recv_sem=recv_sem.at[7],
                    device_id={"gz": lax.rem(me + step, BLOCKS)}, device_id_type=MESH).start()
                return carry

            lax.fori_loop(1, BLOCKS, send_flow, 0)
            flow_in[pl.ds(me * 2, 2)] = flow_out[...]

        def up(j, s):
            now = z_ref[rows8(j)] + g_ref[rows8(j)] * s
            rsend[c, rows8(j + 1)] = jnp.where(upper_half, now, pltpu.roll(s, 4, 0))
            return now

        s = sweep(up, zero, backward=True)
        rsend[c, 0:8] = jnp.where(upper_half, 0.0, pltpu.roll(s, 4, 0))
        send_all(rsend.at[c], ret_ref.at[c], 3 + c)

    solve(0)
    send_all(tsend, tbuf_ref, 6)

    left = edge_low
    for k in range(INNER):
        l_ref[k] = left * inv_ref[k]
        left = left * w_ref[k]
    left, right = l_ref[INNER - 1], w_ref[INNER - 1]
    r_ref[INNER - 1] = right
    for k in range(INNER - 2, -1, -1):
        w = w_ref[k]
        left = l_ref[k] + w * left
        right = w * right
        l_ref[k] = left
        r_ref[k] = right

    solve(1)
    solve(2)

    wait_all(flow_in, 2, recv_sem.at[7])

    def add_up(j, carry):
        return carry[0] + flow_in[j * 2], carry[1] + flow_in[j * 2 + 1]

    line = jnp.zeros((1, 128), F32)
    flow, weight = lax.fori_loop(0, BLOCKS, add_up, (line, line))
    plane_out[0] = flow
    plane_out[1] = weight

    def send_plane(step, carry):
        peer = lax.rem(plane + step, PLANES)
        pltpu.make_async_remote_copy(
            src_ref=plane_out, dst_ref=plane_in.at[pl.ds(plane * 2, 2)],
            send_sem=send_sem.at[8], recv_sem=recv_sem.at[8],
            device_id={"gy": peer}, device_id_type=MESH).start()
        return carry


    @pl.when(plane < PLANES - 1)
    def _():
        pl.semaphore_wait(plane_sem, PLANES - 1 - plane)

    lax.fori_loop(1, PLANES, send_plane, 0)
    plane_in[pl.ds(plane * 2, 2)] = plane_out[...]

    def finish(c):
        wait_all(ret_ref.at[c], MSG, recv_sem.at[3 + c])
        before, own = unpack(ret_ref.at[c], 0), unpack(ret_ref.at[c], 4)
        for k in range(INNER):
            p_ref[c, k] = p_ref[c, k] + l_ref[k] * before + r_ref[k] * own
        p_ref[c, INNER] = own

    finish(0)
    wait_all(tbuf_ref, MSG, recv_sem.at[6])
    before, own = unpack(tbuf_ref, 0), unpack(tbuf_ref, 4)
    for k in range(INNER):
        u_ref[k] = 1.0 - l_ref[k] * before - r_ref[k] * own
    u_ref[INNER] = 1.0 - own
    finish(1)
    finish(2)
    for c in range(3):
        wait_all(fsend.at[c], MSG, send_sem.at[c])
        wait_all(rsend.at[c], MSG, send_sem.at[3 + c])
    wait_all(tsend, MSG, send_sem.at[6])
    wait_all(flow_in, 2, send_sem.at[7])
    span = plane_in.at[pl.ds(0, (PLANES - 1) * 2)]
    pltpu.make_async_copy(span, span, send_sem.at[8]).wait()

    bulk_load.wait()
    span = plane_in.at[pl.ds(0, (PLANES - 1) * 2)]
    pltpu.make_async_copy(span, span, recv_sem.at[8]).wait()
    flow, weight = line, line
    for j in range(PLANES):
        flow = flow + plane_in[2 * j]
        weight = weight + plane_in[2 * j + 1]
    flow = jnp.sum(jnp.broadcast_to(flow, (8, 128)), axis=1, keepdims=True)
    weight = jnp.sum(jnp.broadcast_to(weight, (8, 128)), axis=1, keepdims=True)
    lines = float(PLANES * ROWS * LANES)
    volume = jnp.broadcast_to(column, (8, 128)) * lines
    fix_ref[...] = (bulk_ref[0] * volume - jnp.broadcast_to(flow, (8, 128))) / jnp.broadcast_to(weight, (8, 128))


def unpack(ref, row):
    bands = []
    for a in range(ROWS // 8):
        bands.append(jnp.concatenate(
            [ref[pl.ds(a * 8 * MSG + row + b, 8, stride=MSG), :] for b in range(TILES)], axis=1))
    return jnp.concatenate(bands, axis=0)


def finish_kernel(p_ref, u_ref, fix_ref, out_hbm, out_ref, sem):
    copies = []

    def write(src, dst, start, slot):
        copy = pltpu.make_async_copy(src.at[pl.ds(start, 4)], dst.at[pl.ds(start, 4)], sem.at[slot, start // 4])
        copy.start()
        copies.append(copy)

    for c in (1, 2):
        for start in range(0, CELLS, 4):
            write(p_ref.at[c], out_hbm.at[c], start, c)
    fix = wide(fix_ref[...])
    for k in range(CELLS):
        out_ref[k] = p_ref[0, k] + fix * u_ref[k]
        if k % 4 == 3:
            write(out_ref, out_hbm.at[0], k - 3, 0)
    for copy in copies:
        copy.wait()


def shards(velocity, diffusion, wall_types, stretch_index, bulk_target):
    hbm = pl.BlockSpec(memory_space=pltpu.HBM)
    vmem = pl.BlockSpec(memory_space=pltpu.VMEM)
    plane = (ROWS, LANES)
    mids = pl.pallas_call(
        reduce_kernel,
        name="reduce_and_solve",
        out_shape=[
            pltpu.VMEM((3, CELLS) + plane, F32),
            pltpu.VMEM((CELLS,) + plane, F32),
            pltpu.VMEM((8, 128), F32),
        ],
        in_specs=[hbm] * 5,
        out_specs=[vmem] * 3,
        scratch_shapes=[
            pltpu.VMEM((INNER,) + plane, F32),
            pltpu.VMEM((INNER,) + plane, F32),
            pltpu.VMEM((3, BLOCKS * MSG, 128), F32),
            pltpu.VMEM((BLOCKS * MSG, 128), F32),
            pltpu.VMEM((3, CELLS) + plane, F32),
            pltpu.VMEM(plane, F32),
            pltpu.VMEM(plane, jnp.int32),
            pltpu.SMEM((BLOCKS * CELLS,), jnp.int32),
            pltpu.SMEM((1,), F32),
            pltpu.VMEM((INNER,) + plane, F32),
            pltpu.VMEM((INNER,) + plane, F32),
            pltpu.VMEM((CELLS, BLOCKS, 128), F32),
            pltpu.VMEM((3, BLOCKS * MSG, 128), F32),
            pltpu.VMEM((3, (BLOCKS + 1) * MSG, 128), F32),
            *[pltpu.VMEM(((BLOCKS + 1) * 8, 128), F32)] * 9,
            pltpu.VMEM(((BLOCKS + 1) * MSG, 128), F32),
            pltpu.VMEM((3, (BLOCKS + 1) * MSG, 128), F32),
            pltpu.VMEM((2, 1, 128), F32),
            pltpu.VMEM((BLOCKS * 2, 1, 128), F32),
            pltpu.VMEM((2, 1, 128), F32),
            pltpu.VMEM((PLANES * 2, 1, 128), F32),
            pltpu.SemaphoreType.DMA((4,)),
            pltpu.SemaphoreType.DMA((3,)),
            pltpu.SemaphoreType.DMA((9,)),
            pltpu.SemaphoreType.DMA((9,)),
            pltpu.SemaphoreType.REGULAR,
        ],
        compiler_params=pltpu.CompilerParams(
            collective_id=0, has_side_effects=True, vmem_limit_bytes=24 * 2**20),
    )(*[pltpu.with_memory_space_constraint(x, pltpu.HBM)
        for x in (velocity, diffusion, wall_types, stretch_index)], bulk_target)
    return pl.pallas_call(
        finish_kernel,
        name="finish",
        out_shape=jax.ShapeDtypeStruct((3, CELLS) + plane, F32),
        in_specs=[vmem] * 3,
        out_specs=hbm,
        scratch_shapes=[pltpu.VMEM((CELLS,) + plane, F32), pltpu.SemaphoreType.DMA((3, 4))],
        compiler_params=pltpu.CompilerParams(vmem_limit_bytes=24 * 2**20),
    )(*mids)


def solution(mesh):
    return jax.shard_map(
        shards,
        mesh=mesh,
        in_specs=(P(None, "gz", "gy", None), P("gy", None), P("gy", None), P(), P()),
        out_specs=P(None, "gz", "gy", None),
        check_vma=False,
    )
```

```python
import jax
import jax.numpy as jnp
from jax import lax
from jax.experimental import pallas as pl
from jax.experimental.pallas import tpu as pltpu
from jax.sharding import PartitionSpec as P

MESH = pl.DeviceIdType.MESH
F32 = jnp.float32
BLOCKS = 32
PLANES = 8
CELLS = 16
INNER = CELLS - 1
ROWS = 32
LANES = 512
TILES = LANES // 128
MSG = 8
GROUP = 8


FAR_FIRST = sorted(range(1, BLOCKS), key=lambda i: -min(i // 8, 4 - i // 8) - min(i // 2 % 4, 4 - i // 2 % 4))


def inverse(x):
    guess = pl.reciprocal(x, approx=True)
    return guess * (2.0 - x * guess)


def wide(tile):
    row = jnp.concatenate([tile] * TILES, axis=1)
    return jnp.concatenate([row] * (ROWS // 8), axis=0)


def across(column):
    return jnp.concatenate([column] * TILES, axis=1)


def tiles_of():
    return [(a, b) for a in range(ROWS // 8) for b in range(TILES)]


def part(x, a, b):
    return x[a * 8:(a + 1) * 8, b * 128:(b + 1) * 128]


def reduce_kernel(velocity, diffusion, walls, stretch, bulk,
                  p_ref, u_ref, fix_ref,
                  l_ref, r_ref, ret_ref, tbuf_ref, v_ref, d_ref, wall_ref, stretch_ref, bulk_ref, w_ref, inv_ref, hb_ref,
                  fsend, frecv, al_ref, be_ref, dh_ref, im_ref, a_ref, g_ref, t_ref, z_ref, y_ref,
                  tsend, rsend, flow_out, flow_in, plane_out, plane_in,
                  load_sem, v_sem, send_sem, recv_sem, plane_sem):
    me = lax.axis_index("gz")
    plane = lax.axis_index("gy")

    def load(src, dst, sem):
        copy = pltpu.make_async_copy(src, dst, sem)
        copy.start()
        return copy

    barrier = pltpu.get_barrier_semaphore()

    def greet(step, carry):
        pl.semaphore_signal(barrier, 1, device_id={"gz": lax.rem(me + step, BLOCKS)}, device_id_type=MESH)
        return carry

    def greet_plane(other, carry):
        pl.semaphore_signal(barrier, 1, device_id={"gy": other}, device_id_type=MESH)
        return carry

    lax.fori_loop(1, BLOCKS, greet, 0)
    lax.fori_loop(plane + 1, PLANES, greet_plane, 0)

    stretch_load = load(stretch, stretch_ref, load_sem.at[0])
    d_load = load(diffusion, d_ref, load_sem.at[2])
    wall_load = load(walls, wall_ref, load_sem.at[3])
    v_loads = [load(velocity.at[0], v_ref.at[0], v_sem.at[0])]

    stretch_load.wait()

    def height(cell):
        return 0.5 + 0.25 * stretch_ref[cell].astype(F32)

    first = me * CELLS
    h = [height(first + k) for k in range(CELLS)]
    below = height(jnp.maximum(first - 1, 0))

    def face(one, other):
        return 2.0 * inverse(jnp.full((8, 128), one + other, F32))

    ends = [below] + h
    f = [wide(face(ends[k], ends[k + 1])) for k in range(CELLS)]
    floor_scale = 2.0 * inverse(jnp.full((8, 128), height(0), F32))
    roof_scale = 2.0 * inverse(jnp.full((8, 128), height(BLOCKS * CELLS - 1), F32))
    d_load.wait()
    wall_load.wait()
    v_loads += [load(velocity.at[c], v_ref.at[c], v_sem.at[c]) for c in (1, 2)]
    bulk_load = load(bulk, bulk_ref, load_sem.at[1])
    d = d_ref[...]
    lower_wall = (wall_ref[...] & 1).astype(F32) * wide(floor_scale)
    edge_low = d * jnp.where(me == 0, lower_wall, f[0])

    w = None
    low = edge_low
    for k in range(INNER):
        high = d * f[k + 1]
        pivot = h[k] + (low + high)
        if k:
            pivot = pivot - low * w
        inv = inverse(pivot)
        w = high * inv
        low = high
        inv_ref[k] = inv
        w_ref[k] = w
    edge_high = low

    def send_all(src, dst, which):
        x, y, core = me // 8, lax.rem(me // 2, 4), lax.rem(me, 2)

        for step in FAR_FIRST:
            peer = lax.rem(x + step // 8, 4) * 8 + lax.rem(y + (step // 2) % 4, 4) * 2 + (lax.rem(core + step % 2, 2))
            pltpu.make_async_remote_copy(
                src_ref=src.at[pl.ds(pl.multiple_of(peer * MSG, MSG), MSG)],
                dst_ref=dst.at[pl.ds(pl.multiple_of(me * MSG, MSG), MSG)],
                send_sem=send_sem.at[which], recv_sem=recv_sem.at[which],
                device_id={"gz": peer}, device_id_type=MESH).start()
        mine = pl.ds(pl.multiple_of(me * MSG, MSG), MSG)
        dst[mine] = src[mine]

    def wait_all(ref, rows, sem):
        span = ref.at[pl.ds(0, (BLOCKS - 1) * rows)]
        pltpu.make_async_copy(span, span, sem).wait()

    def answer_plane(other, carry):
        pl.semaphore_signal(plane_sem, 1, device_id={"gy": other}, device_id_type=MESH)
        return carry

    total = jnp.zeros((ROWS, LANES), F32)
    for c in range(3):
        v_loads[c].wait()
        y = None
        for k in range(INNER):
            rhs = h[k] * v_ref[c, k]
            if c == 0:
                total = total + rhs
            y = rhs if k == 0 else rhs + w_ref[k - 1] * y
            p_ref[c, k] = y
        x = inv_ref[INNER - 1] * y
        p_ref[c, INNER - 1] = x
        own = h[INNER] * v_ref[c, INNER]
        if c == 0:
            total = total + own
        own = own + edge_high * x
        for k in range(INNER - 2, -1, -1):
            x = inv_ref[k] * p_ref[c, k] + w_ref[k] * x
            p_ref[c, k] = x
        other = edge_low * x
        for a, b in tiles_of():
            at = a * 8 * MSG + b
            fsend[c, pl.ds(at, 8, stride=MSG), :] = part(own, a, b)
            fsend[c, pl.ds(at + 4, 8, stride=MSG), :] = part(other, a, b)
        if c == 0:
            pl.semaphore_wait(barrier, BLOCKS - 1 + plane)
        send_all(fsend.at[c], frecv.at[c], c)
        if c == 0:
            lax.fori_loop(0, plane, answer_plane, 0)
    local = jnp.zeros((8, 128), F32)
    for a, b in tiles_of():
        local = local + part(total, a, b)

    def table_row(block, carry):
        for k in range(CELLS):
            hb_ref[k, pl.ds(block, 1), :] = jnp.full((1, 128), height(block * CELLS + k), F32)
        return carry

    lax.fori_loop(0, BLOCKS, table_row, 0)
    block_id = lax.broadcasted_iota(jnp.int32, (BLOCKS, LANES), 0)
    heights = [hb_ref[k] for k in range(CELLS)]
    before = pltpu.roll(heights[INNER], 1, 0)
    after = pltpu.roll(heights[0], BLOCKS - 1, 0)
    ends = [before] + heights + [after]
    faces = [across(2.0 * inverse(ends[k] + ends[k + 1])) for k in range(CELLS + 1)]
    row_d = d_ref[pl.ds(me, 1), :]
    row_wall = wall_ref[pl.ds(me, 1), :]
    row_low = (row_wall & 1).astype(F32) * across(floor_scale[0:1])
    row_high = (row_wall >> 1).astype(F32) * across(roof_scale[0:1])
    faces[0] = jnp.where(block_id == 0, row_low, faces[0])
    faces[CELLS] = jnp.where(block_id == BLOCKS - 1, row_high, faces[CELLS])
    dd = jnp.broadcast_to(row_d, (BLOCKS, LANES))
    w = None
    q = dd * faces[0]
    first_edge = q
    alpha = None
    for k in range(INNER):
        low, high = dd * faces[k], dd * faces[k + 1]
        pivot = across(heights[k]) + (low + high)
        if k:
            pivot = pivot - low * w
        inv = inverse(pivot)
        w = high * inv
        gain = q * q * inv
        alpha = gain if alpha is None else alpha + gain
        q = q * w
    high = dd * faces[INNER]
    last_edge = dd * faces[CELLS]
    own_diagonal = across(heights[INNER]) + (high + last_edge) - high * w
    for a, b in tiles_of():
        for half in (0, 4):
            at = pl.ds(a * 64 + b + half, 8, stride=8)
            al_ref[at, :] = part(alpha, a, b)
            be_ref[at, :] = part(q, a, b)
            dh_ref[at, :] = part(own_diagonal, a, b)
    for b in range(TILES):
        for half in (0, 4):
            z_ref[pl.ds(b + half, 8, stride=8), :] = part(first_edge, 0, b)
            y_ref[pl.ds(b + half, 8, stride=8), :] = part(last_edge, BLOCKS // 8 - 1, b)
    floor_edge = z_ref[0:8]
    roof_edge = y_ref[56:64]
    zero = jnp.zeros((8, 128), F32)
    one = jnp.ones((8, 128), F32)
    al_ref[256:264] = zero
    be_ref[256:264] = zero
    low_lanes = lax.broadcasted_iota(jnp.int32, (8, 128), 1) < 64
    upper_half = lax.broadcasted_iota(jnp.int32, (8, 128), 0) < 4

    def rows8(at):
        return pl.ds(pl.multiple_of(at * 8, 8), 8)

    def sweep(step, carry, backward=False):
        def group(at, carry):
            for u in range(GROUP):
                j = at * GROUP + u
                carry = step(BLOCKS - 1 - j if backward else j, carry)
            return carry
        return lax.fori_loop(0, BLOCKS // GROUP, group, carry)

    def factor(j, carry):
        g, z = carry
        beta = be_ref[rows8(j)]
        pivot = dh_ref[rows8(j)] - al_ref[rows8(j + 1)] - beta * g
        im = inverse(pivot)
        a = beta * im
        g = be_ref[rows8(j + 1)] * im
        z = a * z
        im_ref[rows8(j)] = im
        a_ref[rows8(j)] = a
        g_ref[rows8(j)] = g
        z_ref[rows8(j)] = z
        return g, z

    sweep(factor, (zero, one))
    last = pl.ds((BLOCKS - 1) * 8, 8)
    z_ref[last] = z_ref[last] + roof_edge * im_ref[last]

    def unit_back(j, t):
        now = z_ref[rows8(j)] + g_ref[rows8(j)] * t
        t_ref[rows8(j)] = now
        tsend[rows8(j + 1)] = jnp.where(upper_half, now, t)
        return now

    t = sweep(unit_back, zero, backward=True)
    tsend[0:8] = jnp.where(upper_half, one, t)
    height_sum = heights[0]
    for k in range(1, CELLS):
        height_sum = height_sum + heights[k]
    column = jnp.sum(height_sum, axis=0, keepdims=True)
    weight = column - (floor_edge - al_ref[0:8] - be_ref[0:8] * t) - roof_edge * (1.0 - t_ref[last])

    def solve(c):
        frecv[c, pl.ds(BLOCKS * MSG, MSG)] = zero
        wait_all(frecv.at[c], MSG, recv_sem.at[c])

        def down(j, carry):
            z, flow = carry
            rho = frecv[c, rows8(j)] + pltpu.roll(frecv[c, rows8(j + 1)], 4, 0)
            if c == 0:
                flow = flow + rho * t_ref[rows8(j)]
            z = rho * im_ref[rows8(j)] + a_ref[rows8(j)] * z
            z_ref[rows8(j)] = z
            return z, flow

        _, flow = sweep(down, (zero, pltpu.roll(frecv[c, 0:8], 4, 0)))
        if c == 0:
            sums = local + pltpu.roll(local, 4, 0)
            flow = jnp.sum(jnp.where(upper_half, sums - flow, 0.0), axis=0, keepdims=True)
            unit = jnp.sum(jnp.where(upper_half, weight, 0.0), axis=0, keepdims=True)
            flow = flow + pltpu.roll(flow, 64, 1)
            unit = unit + pltpu.roll(unit, 64, 1)
            flow_out[0] = jnp.where(low_lanes[0:1], flow, unit)

            def send_flow(step, carry):
                pltpu.make_async_remote_copy(
                    src_ref=flow_out, dst_ref=flow_in.at[pl.ds(me, 1)],
                    send_sem=send_sem.at[7], recv_sem=recv_sem.at[7],
                    device_id={"gz": lax.rem(me + step, BLOCKS)}, device_id_type=MESH).start()
                return carry

            lax.fori_loop(1, BLOCKS, send_flow, 0)
            flow_in[pl.ds(me, 1)] = flow_out[...]

        def up(j, s):
            now = z_ref[rows8(j)] + g_ref[rows8(j)] * s
            rsend[c, rows8(j + 1)] = jnp.where(upper_half, now, pltpu.roll(s, 4, 0))
            return now

        s = sweep(up, zero, backward=True)
        rsend[c, 0:8] = jnp.where(upper_half, 0.0, pltpu.roll(s, 4, 0))
        send_all(rsend.at[c], ret_ref.at[c], 3 + c)

    send_all(tsend, tbuf_ref, 6)
    solve(0)

    left = edge_low
    for k in range(INNER):
        l_ref[k] = left * inv_ref[k]
        left = left * w_ref[k]
    left, right = l_ref[INNER - 1], w_ref[INNER - 1]
    r_ref[INNER - 1] = right
    for k in range(INNER - 2, -1, -1):
        w = w_ref[k]
        left = l_ref[k] + w * left
        right = w * right
        l_ref[k] = left
        r_ref[k] = right

    solve(1)
    solve(2)

    wait_all(flow_in, 1, recv_sem.at[7])

    parts = [flow_in[j] for j in range(BLOCKS)]
    while len(parts) > 1:
        parts = [parts[2 * j] + parts[2 * j + 1] for j in range(len(parts) // 2)]
    plane_out[0] = parts[0]

    def send_plane(step, carry):
        peer = lax.rem(plane + step, PLANES)
        pltpu.make_async_remote_copy(
            src_ref=plane_out, dst_ref=plane_in.at[pl.ds(plane, 1)],
            send_sem=send_sem.at[8], recv_sem=recv_sem.at[8],
            device_id={"gy": peer}, device_id_type=MESH).start()
        return carry


    @pl.when(plane < PLANES - 1)
    def _():
        pl.semaphore_wait(plane_sem, PLANES - 1 - plane)

    lax.fori_loop(1, PLANES, send_plane, 0)
    plane_in[pl.ds(plane, 1)] = plane_out[...]

    def finish(c):
        wait_all(ret_ref.at[c], MSG, recv_sem.at[3 + c])
        before, own = unpack(ret_ref.at[c], 0), unpack(ret_ref.at[c], 4)
        for k in range(INNER):
            p_ref[c, k] = p_ref[c, k] + l_ref[k] * before + r_ref[k] * own
        p_ref[c, INNER] = own

    finish(0)
    wait_all(tbuf_ref, MSG, recv_sem.at[6])
    before, own = unpack(tbuf_ref, 0), unpack(tbuf_ref, 4)
    for k in range(INNER):
        u_ref[k] = 1.0 - l_ref[k] * before - r_ref[k] * own
    u_ref[INNER] = 1.0 - own
    finish(1)
    finish(2)
    for c in range(3):
        wait_all(fsend.at[c], MSG, send_sem.at[c])
        wait_all(rsend.at[c], MSG, send_sem.at[3 + c])
    wait_all(tsend, MSG, send_sem.at[6])
    wait_all(flow_in, 1, send_sem.at[7])
    span = plane_in.at[pl.ds(0, PLANES - 1)]
    pltpu.make_async_copy(span, span, send_sem.at[8]).wait()

    bulk_load.wait()
    span = plane_in.at[pl.ds(0, PLANES - 1)]
    pltpu.make_async_copy(span, span, recv_sem.at[8]).wait()
    parts = [plane_in[j] for j in range(PLANES)]
    while len(parts) > 1:
        parts = [parts[2 * j] + parts[2 * j + 1] for j in range(len(parts) // 2)]
    sums = jnp.broadcast_to(parts[0], (8, 128))
    flow = jnp.sum(jnp.where(low_lanes, sums, 0.0), axis=1, keepdims=True)
    weight = jnp.sum(jnp.where(low_lanes, 0.0, sums), axis=1, keepdims=True)
    lines = float(PLANES * ROWS * LANES)
    volume = jnp.broadcast_to(column, (8, 128)) * lines
    fix_ref[...] = (bulk_ref[0] * volume - jnp.broadcast_to(flow, (8, 128))) / jnp.broadcast_to(weight, (8, 128))


def unpack(ref, row):
    bands = []
    for a in range(ROWS // 8):
        bands.append(jnp.concatenate(
            [ref[pl.ds(a * 8 * MSG + row + b, 8, stride=MSG), :] for b in range(TILES)], axis=1))
    return jnp.concatenate(bands, axis=0)


def finish_kernel(p_ref, u_ref, fix_ref, out_hbm, out_ref, sem):
    copies = []

    def write(src, dst, start, slot):
        copy = pltpu.make_async_copy(src.at[pl.ds(start, 4)], dst.at[pl.ds(start, 4)], sem.at[slot, start // 4])
        copy.start()
        copies.append(copy)

    for c in (1, 2):
        for start in range(0, CELLS, 4):
            write(p_ref.at[c], out_hbm.at[c], start, c)
    fix = wide(fix_ref[...])
    for k in range(CELLS):
        out_ref[k] = p_ref[0, k] + fix * u_ref[k]
        if k % 4 == 3:
            write(out_ref, out_hbm.at[0], k - 3, 0)
    for copy in copies:
        copy.wait()


def shards(velocity, diffusion, wall_types, stretch_index, bulk_target):
    hbm = pl.BlockSpec(memory_space=pltpu.HBM)
    vmem = pl.BlockSpec(memory_space=pltpu.VMEM)
    plane = (ROWS, LANES)
    mids = pl.pallas_call(
        reduce_kernel,
        name="reduce_and_solve",
        out_shape=[
            pltpu.VMEM((3, CELLS) + plane, F32),
            pltpu.VMEM((CELLS,) + plane, F32),
            pltpu.VMEM((8, 128), F32),
        ],
        in_specs=[hbm] * 5,
        out_specs=[vmem] * 3,
        scratch_shapes=[
            pltpu.VMEM((INNER,) + plane, F32),
            pltpu.VMEM((INNER,) + plane, F32),
            pltpu.VMEM((3, BLOCKS * MSG, 128), F32),
            pltpu.VMEM((BLOCKS * MSG, 128), F32),
            pltpu.VMEM((3, CELLS) + plane, F32),
            pltpu.VMEM(plane, F32),
            pltpu.VMEM(plane, jnp.int32),
            pltpu.SMEM((BLOCKS * CELLS,), jnp.int32),
            pltpu.SMEM((1,), F32),
            pltpu.VMEM((INNER,) + plane, F32),
            pltpu.VMEM((INNER,) + plane, F32),
            pltpu.VMEM((CELLS, BLOCKS, 128), F32),
            pltpu.VMEM((3, BLOCKS * MSG, 128), F32),
            pltpu.VMEM((3, (BLOCKS + 1) * MSG, 128), F32),
            *[pltpu.VMEM(((BLOCKS + 1) * 8, 128), F32)] * 9,
            pltpu.VMEM(((BLOCKS + 1) * MSG, 128), F32),
            pltpu.VMEM((3, (BLOCKS + 1) * MSG, 128), F32),
            pltpu.VMEM((1, 1, 128), F32),
            pltpu.VMEM((BLOCKS, 1, 128), F32),
            pltpu.VMEM((1, 1, 128), F32),
            pltpu.VMEM((PLANES, 1, 128), F32),
            pltpu.SemaphoreType.DMA((4,)),
            pltpu.SemaphoreType.DMA((3,)),
            pltpu.SemaphoreType.DMA((9,)),
            pltpu.SemaphoreType.DMA((9,)),
            pltpu.SemaphoreType.REGULAR,
        ],
        compiler_params=pltpu.CompilerParams(
            collective_id=0, has_side_effects=True, vmem_limit_bytes=24 * 2**20),
    )(*[pltpu.with_memory_space_constraint(x, pltpu.HBM)
        for x in (velocity, diffusion, wall_types, stretch_index)], bulk_target)
    return pl.pallas_call(
        finish_kernel,
        name="finish",
        out_shape=jax.ShapeDtypeStruct((3, CELLS) + plane, F32),
        in_specs=[vmem] * 3,
        out_specs=hbm,
        scratch_shapes=[pltpu.VMEM((CELLS,) + plane, F32), pltpu.SemaphoreType.DMA((3, 4))],
        compiler_params=pltpu.CompilerParams(vmem_limit_bytes=24 * 2**20),
    )(*mids)


def solution(mesh):
    return jax.shard_map(
        shards,
        mesh=mesh,
        in_specs=(P(None, "gz", "gy", None), P("gy", None), P("gy", None), P(), P()),
        out_specs=P(None, "gz", "gy", None),
        check_vma=False,
    )
```

```python
import jax
import jax.numpy as jnp
from jax import lax
from jax.experimental import pallas as pl
from jax.experimental.pallas import tpu as pltpu
from jax.sharding import PartitionSpec as P

MESH = pl.DeviceIdType.MESH
F32 = jnp.float32
BLOCKS = 32
PLANES = 8
CELLS = 16
INNER = CELLS - 1
ROWS = 32
LANES = 512
TILES = LANES // 128
MSG = 8
GROUP = 8


FAR_FIRST = sorted(range(1, BLOCKS), key=lambda i: -min(i // 8, 4 - i // 8) - min(i // 2 % 4, 4 - i // 2 % 4))


def inverse(x):
    guess = pl.reciprocal(x, approx=True)
    return guess * (2.0 - x * guess)


def wide(tile):
    row = jnp.concatenate([tile] * TILES, axis=1)
    return jnp.concatenate([row] * (ROWS // 8), axis=0)


def across(column):
    return jnp.concatenate([column] * TILES, axis=1)


def tiles_of():
    return [(a, b) for a in range(ROWS // 8) for b in range(TILES)]


def part(x, a, b):
    return x[a * 8:(a + 1) * 8, b * 128:(b + 1) * 128]


def reduce_kernel(velocity, diffusion, walls, stretch, bulk,
                  p_ref, u_ref, fix_ref,
                  l_ref, r_ref, ret_ref, tbuf_ref, v_ref, d_ref, wall_ref, stretch_ref, bulk_ref, w_ref, inv_ref, hb_ref,
                  fsend, frecv, al_ref, be_ref, dh_ref, im_ref, a_ref, g_ref, t_ref, z_ref, y_ref,
                  tsend, rsend, flow_out, flow_in, plane_out, plane_in,
                  load_sem, v_sem, send_sem, recv_sem, plane_sem):
    me = lax.axis_index("gz")
    plane = lax.axis_index("gy")

    def load(src, dst, sem):
        copy = pltpu.make_async_copy(src, dst, sem)
        copy.start()
        return copy

    barrier = pltpu.get_barrier_semaphore()

    def greet(step, carry):
        pl.semaphore_signal(barrier, 1, device_id={"gz": lax.rem(me + step, BLOCKS)}, device_id_type=MESH)
        return carry

    def greet_plane(other, carry):
        pl.semaphore_signal(barrier, 1, device_id={"gy": other}, device_id_type=MESH)
        return carry

    lax.fori_loop(1, BLOCKS, greet, 0)
    lax.fori_loop(plane + 1, PLANES, greet_plane, 0)

    stretch_load = load(stretch, stretch_ref, load_sem.at[0])
    d_load = load(diffusion, d_ref, load_sem.at[2])
    wall_load = load(walls, wall_ref, load_sem.at[3])
    v_loads = [load(velocity.at[0], v_ref.at[0], v_sem.at[0])]

    stretch_load.wait()

    def height(cell):
        return 0.5 + 0.25 * stretch_ref[cell].astype(F32)

    first = me * CELLS
    h = [height(first + k) for k in range(CELLS)]
    below = height(jnp.maximum(first - 1, 0))

    def face(one, other):
        return 2.0 * inverse(jnp.full((8, 128), one + other, F32))

    ends = [below] + h
    f = [wide(face(ends[k], ends[k + 1])) for k in range(CELLS)]
    floor_scale = 2.0 * inverse(jnp.full((8, 128), height(0), F32))
    roof_scale = 2.0 * inverse(jnp.full((8, 128), height(BLOCKS * CELLS - 1), F32))
    d_load.wait()
    wall_load.wait()
    v_loads += [load(velocity.at[c], v_ref.at[c], v_sem.at[c]) for c in (1, 2)]
    bulk_load = load(bulk, bulk_ref, load_sem.at[1])
    d = d_ref[...]
    lower_wall = (wall_ref[...] & 1).astype(F32) * wide(floor_scale)
    edge_low = d * jnp.where(me == 0, lower_wall, f[0])

    w = None
    low = edge_low
    for k in range(INNER):
        high = d * f[k + 1]
        pivot = h[k] + (low + high)
        if k:
            pivot = pivot - low * w
        inv = inverse(pivot)
        w = high * inv
        low = high
        inv_ref[k] = inv
        w_ref[k] = w
    edge_high = low

    def send_all(src, dst, which):
        x, y, core = me // 8, lax.rem(me // 2, 4), lax.rem(me, 2)

        for step in FAR_FIRST:
            peer = lax.rem(x + step // 8, 4) * 8 + lax.rem(y + (step // 2) % 4, 4) * 2 + (lax.rem(core + step % 2, 2))
            pltpu.make_async_remote_copy(
                src_ref=src.at[pl.ds(pl.multiple_of(peer * MSG, MSG), MSG)],
                dst_ref=dst.at[pl.ds(pl.multiple_of(me * MSG, MSG), MSG)],
                send_sem=send_sem.at[which], recv_sem=recv_sem.at[which],
                device_id={"gz": peer}, device_id_type=MESH).start()
        mine = pl.ds(pl.multiple_of(me * MSG, MSG), MSG)
        dst[mine] = src[mine]

    def wait_all(ref, rows, sem):
        span = ref.at[pl.ds(0, (BLOCKS - 1) * rows)]
        pltpu.make_async_copy(span, span, sem).wait()

    def answer_plane(other, carry):
        pl.semaphore_signal(plane_sem, 1, device_id={"gy": other}, device_id_type=MESH)
        return carry

    total = jnp.zeros((ROWS, LANES), F32)
    for c in range(3):
        v_loads[c].wait()
        y = None
        for k in range(INNER):
            rhs = h[k] * v_ref[c, k]
            if c == 0:
                total = total + rhs
            y = rhs if k == 0 else rhs + w_ref[k - 1] * y
            p_ref[c, k] = y
        x = inv_ref[INNER - 1] * y
        p_ref[c, INNER - 1] = x
        own = h[INNER] * v_ref[c, INNER]
        if c == 0:
            total = total + own
        own = own + edge_high * x
        for k in range(INNER - 2, -1, -1):
            x = inv_ref[k] * p_ref[c, k] + w_ref[k] * x
            p_ref[c, k] = x
        other = edge_low * x
        for a, b in tiles_of():
            at = a * 8 * MSG + b
            fsend[c, pl.ds(at, 8, stride=MSG), :] = part(own, a, b)
            fsend[c, pl.ds(at + 4, 8, stride=MSG), :] = part(other, a, b)

    pl.semaphore_wait(barrier, BLOCKS - 1 + plane)
    for c in range(3):
        send_all(fsend.at[c], frecv.at[c], c)
    lax.fori_loop(0, plane, answer_plane, 0)
    local = jnp.zeros((8, 128), F32)
    for a, b in tiles_of():
        local = local + part(total, a, b)

    def table_row(block, carry):
        for k in range(CELLS):
            hb_ref[k, pl.ds(block, 1), :] = jnp.full((1, 128), height(block * CELLS + k), F32)
        return carry

    lax.fori_loop(0, BLOCKS, table_row, 0)
    block_id = lax.broadcasted_iota(jnp.int32, (BLOCKS, LANES), 0)
    heights = [hb_ref[k] for k in range(CELLS)]
    before = pltpu.roll(heights[INNER], 1, 0)
    after = pltpu.roll(heights[0], BLOCKS - 1, 0)
    ends = [before] + heights + [after]
    faces = [across(2.0 * inverse(ends[k] + ends[k + 1])) for k in range(CELLS + 1)]
    row_d = d_ref[pl.ds(me, 1), :]
    row_wall = wall_ref[pl.ds(me, 1), :]
    row_low = (row_wall & 1).astype(F32) * across(floor_scale[0:1])
    row_high = (row_wall >> 1).astype(F32) * across(roof_scale[0:1])
    faces[0] = jnp.where(block_id == 0, row_low, faces[0])
    faces[CELLS] = jnp.where(block_id == BLOCKS - 1, row_high, faces[CELLS])
    dd = jnp.broadcast_to(row_d, (BLOCKS, LANES))
    w = None
    q = dd * faces[0]
    first_edge = q
    alpha = None
    for k in range(INNER):
        low, high = dd * faces[k], dd * faces[k + 1]
        pivot = across(heights[k]) + (low + high)
        if k:
            pivot = pivot - low * w
        inv = inverse(pivot)
        w = high * inv
        gain = q * q * inv
        alpha = gain if alpha is None else alpha + gain
        q = q * w
    high = dd * faces[INNER]
    last_edge = dd * faces[CELLS]
    own_diagonal = across(heights[INNER]) + (high + last_edge) - high * w
    for a, b in tiles_of():
        for half in (0, 4):
            at = pl.ds(a * 64 + b + half, 8, stride=8)
            al_ref[at, :] = part(alpha, a, b)
            be_ref[at, :] = part(q, a, b)
            dh_ref[at, :] = part(own_diagonal, a, b)
    for b in range(TILES):
        for half in (0, 4):
            z_ref[pl.ds(b + half, 8, stride=8), :] = part(first_edge, 0, b)
            y_ref[pl.ds(b + half, 8, stride=8), :] = part(last_edge, BLOCKS // 8 - 1, b)
    floor_edge = z_ref[0:8]
    roof_edge = y_ref[56:64]
    zero = jnp.zeros((8, 128), F32)
    one = jnp.ones((8, 128), F32)
    al_ref[256:264] = zero
    be_ref[256:264] = zero
    low_lanes = lax.broadcasted_iota(jnp.int32, (8, 128), 1) < 64
    upper_half = lax.broadcasted_iota(jnp.int32, (8, 128), 0) < 4

    def rows8(at):
        return pl.ds(pl.multiple_of(at * 8, 8), 8)

    def sweep(step, carry, backward=False):
        def group(at, carry):
            for u in range(GROUP):
                j = at * GROUP + u
                carry = step(BLOCKS - 1 - j if backward else j, carry)
            return carry
        return lax.fori_loop(0, BLOCKS // GROUP, group, carry)

    def factor(j, carry):
        g, z = carry
        beta = be_ref[rows8(j)]
        pivot = dh_ref[rows8(j)] - al_ref[rows8(j + 1)] - beta * g
        im = inverse(pivot)
        a = beta * im
        g = be_ref[rows8(j + 1)] * im
        z = a * z
        im_ref[rows8(j)] = im
        a_ref[rows8(j)] = a
        g_ref[rows8(j)] = g
        z_ref[rows8(j)] = z
        return g, z

    sweep(factor, (zero, one))
    last = pl.ds((BLOCKS - 1) * 8, 8)
    z_ref[last] = z_ref[last] + roof_edge * im_ref[last]

    def unit_back(j, t):
        now = z_ref[rows8(j)] + g_ref[rows8(j)] * t
        t_ref[rows8(j)] = now
        tsend[rows8(j + 1)] = jnp.where(upper_half, now, t)
        return now

    t = sweep(unit_back, zero, backward=True)
    tsend[0:8] = jnp.where(upper_half, one, t)
    height_sum = heights[0]
    for k in range(1, CELLS):
        height_sum = height_sum + heights[k]
    column = jnp.sum(height_sum, axis=0, keepdims=True)
    weight = column - (floor_edge - al_ref[0:8] - be_ref[0:8] * t) - roof_edge * (1.0 - t_ref[last])

    def solve(c):
        frecv[c, pl.ds(BLOCKS * MSG, MSG)] = zero
        wait_all(frecv.at[c], MSG, recv_sem.at[c])

        def rhs(j):
            return frecv[c, rows8(j)] + pltpu.roll(frecv[c, rows8(j + 1)], 4, 0)

        if c == 0:
            flow = sweep(lambda j, flow: flow + rhs(j) * t_ref[rows8(j)], pltpu.roll(frecv[0, 0:8], 4, 0))
            sums = local + pltpu.roll(local, 4, 0)
            flow = jnp.sum(jnp.where(upper_half, sums - flow, 0.0), axis=0, keepdims=True)
            unit = jnp.sum(jnp.where(upper_half, weight, 0.0), axis=0, keepdims=True)
            flow = flow + pltpu.roll(flow, 64, 1)
            unit = unit + pltpu.roll(unit, 64, 1)
            flow_out[0] = jnp.where(low_lanes[0:1], flow, unit)

            def send_flow(step, carry):
                pltpu.make_async_remote_copy(
                    src_ref=flow_out, dst_ref=flow_in.at[pl.ds(me, 1)],
                    send_sem=send_sem.at[7], recv_sem=recv_sem.at[7],
                    device_id={"gz": lax.rem(me + step, BLOCKS)}, device_id_type=MESH).start()
                return carry

            lax.fori_loop(1, BLOCKS, send_flow, 0)
            flow_in[pl.ds(me, 1)] = flow_out[...]

        def down(j, z):
            z = rhs(j) * im_ref[rows8(j)] + a_ref[rows8(j)] * z
            z_ref[rows8(j)] = z
            return z

        sweep(down, zero)

        def up(j, s):
            now = z_ref[rows8(j)] + g_ref[rows8(j)] * s
            rsend[c, rows8(j + 1)] = jnp.where(upper_half, now, pltpu.roll(s, 4, 0))
            return now

        s = sweep(up, zero, backward=True)
        rsend[c, 0:8] = jnp.where(upper_half, 0.0, pltpu.roll(s, 4, 0))
        send_all(rsend.at[c], ret_ref.at[c], 3 + c)

    send_all(tsend, tbuf_ref, 6)
    solve(0)

    left = edge_low
    for k in range(INNER):
        l_ref[k] = left * inv_ref[k]
        left = left * w_ref[k]
    left, right = l_ref[INNER - 1], w_ref[INNER - 1]
    r_ref[INNER - 1] = right
    for k in range(INNER - 2, -1, -1):
        w = w_ref[k]
        left = l_ref[k] + w * left
        right = w * right
        l_ref[k] = left
        r_ref[k] = right

    solve(1)
    solve(2)

    wait_all(flow_in, 1, recv_sem.at[7])

    parts = [flow_in[j] for j in range(BLOCKS)]
    while len(parts) > 1:
        parts = [parts[2 * j] + parts[2 * j + 1] for j in range(len(parts) // 2)]
    plane_out[0] = parts[0]

    def send_plane(step, carry):
        peer = lax.rem(plane + step, PLANES)
        pltpu.make_async_remote_copy(
            src_ref=plane_out, dst_ref=plane_in.at[pl.ds(plane, 1)],
            send_sem=send_sem.at[8], recv_sem=recv_sem.at[8],
            device_id={"gy": peer}, device_id_type=MESH).start()
        return carry


    @pl.when(plane < PLANES - 1)
    def _():
        pl.semaphore_wait(plane_sem, PLANES - 1 - plane)

    lax.fori_loop(1, PLANES, send_plane, 0)
    plane_in[pl.ds(plane, 1)] = plane_out[...]

    def finish(c):
        wait_all(ret_ref.at[c], MSG, recv_sem.at[3 + c])
        before, own = unpack(ret_ref.at[c], 0), unpack(ret_ref.at[c], 4)
        for k in range(INNER):
            p_ref[c, k] = p_ref[c, k] + l_ref[k] * before + r_ref[k] * own
        p_ref[c, INNER] = own

    finish(0)
    wait_all(tbuf_ref, MSG, recv_sem.at[6])
    before, own = unpack(tbuf_ref, 0), unpack(tbuf_ref, 4)
    for k in range(INNER):
        u_ref[k] = 1.0 - l_ref[k] * before - r_ref[k] * own
    u_ref[INNER] = 1.0 - own
    finish(1)
    finish(2)
    for c in range(3):
        wait_all(fsend.at[c], MSG, send_sem.at[c])
        wait_all(rsend.at[c], MSG, send_sem.at[3 + c])
    wait_all(tsend, MSG, send_sem.at[6])
    wait_all(flow_in, 1, send_sem.at[7])
    span = plane_in.at[pl.ds(0, PLANES - 1)]
    pltpu.make_async_copy(span, span, send_sem.at[8]).wait()

    bulk_load.wait()
    span = plane_in.at[pl.ds(0, PLANES - 1)]
    pltpu.make_async_copy(span, span, recv_sem.at[8]).wait()
    parts = [plane_in[j] for j in range(PLANES)]
    while len(parts) > 1:
        parts = [parts[2 * j] + parts[2 * j + 1] for j in range(len(parts) // 2)]
    sums = jnp.broadcast_to(parts[0], (8, 128))
    flow = jnp.sum(jnp.where(low_lanes, sums, 0.0), axis=1, keepdims=True)
    weight = jnp.sum(jnp.where(low_lanes, 0.0, sums), axis=1, keepdims=True)
    lines = float(PLANES * ROWS * LANES)
    volume = jnp.broadcast_to(column, (8, 128)) * lines
    fix_ref[...] = (bulk_ref[0] * volume - jnp.broadcast_to(flow, (8, 128))) / jnp.broadcast_to(weight, (8, 128))


def unpack(ref, row):
    bands = []
    for a in range(ROWS // 8):
        bands.append(jnp.concatenate(
            [ref[pl.ds(a * 8 * MSG + row + b, 8, stride=MSG), :] for b in range(TILES)], axis=1))
    return jnp.concatenate(bands, axis=0)


def finish_kernel(p_ref, u_ref, fix_ref, out_hbm, out_ref, sem):
    copies = []

    def write(src, dst, start, slot):
        copy = pltpu.make_async_copy(src.at[pl.ds(start, 4)], dst.at[pl.ds(start, 4)], sem.at[slot, start // 4])
        copy.start()
        copies.append(copy)

    for c in (1, 2):
        for start in range(0, CELLS, 4):
            write(p_ref.at[c], out_hbm.at[c], start, c)
    fix = wide(fix_ref[...])
    for k in range(CELLS):
        out_ref[k] = p_ref[0, k] + fix * u_ref[k]
        if k % 4 == 3:
            write(out_ref, out_hbm.at[0], k - 3, 0)
    for copy in copies:
        copy.wait()


def shards(velocity, diffusion, wall_types, stretch_index, bulk_target):
    hbm = pl.BlockSpec(memory_space=pltpu.HBM)
    vmem = pl.BlockSpec(memory_space=pltpu.VMEM)
    plane = (ROWS, LANES)
    mids = pl.pallas_call(
        reduce_kernel,
        name="reduce_and_solve",
        out_shape=[
            pltpu.VMEM((3, CELLS) + plane, F32),
            pltpu.VMEM((CELLS,) + plane, F32),
            pltpu.VMEM((8, 128), F32),
        ],
        in_specs=[hbm] * 5,
        out_specs=[vmem] * 3,
        scratch_shapes=[
            pltpu.VMEM((INNER,) + plane, F32),
            pltpu.VMEM((INNER,) + plane, F32),
            pltpu.VMEM((3, (BLOCKS + 1) * MSG, 128), F32),
            pltpu.VMEM(((BLOCKS + 1) * MSG, 128), F32),
            pltpu.VMEM((3, CELLS) + plane, F32),
            pltpu.VMEM(plane, F32),
            pltpu.VMEM(plane, jnp.int32),
            pltpu.SMEM((BLOCKS * CELLS,), jnp.int32),
            pltpu.SMEM((1,), F32),
            pltpu.VMEM((INNER,) + plane, F32),
            pltpu.VMEM((INNER,) + plane, F32),
            pltpu.VMEM((CELLS, BLOCKS, 128), F32),
            pltpu.VMEM((3, (BLOCKS + 1) * MSG, 128), F32),
            pltpu.VMEM((3, (BLOCKS + 1) * MSG, 128), F32),
            *[pltpu.VMEM(((BLOCKS + 1) * 8, 128), F32)] * 9,
            pltpu.VMEM(((BLOCKS + 1) * MSG, 128), F32),
            pltpu.VMEM((3, (BLOCKS + 1) * MSG, 128), F32),
            pltpu.VMEM((1, 1, 128), F32),
            pltpu.VMEM((BLOCKS, 1, 128), F32),
            pltpu.VMEM((1, 1, 128), F32),
            pltpu.VMEM((PLANES, 1, 128), F32),
            pltpu.SemaphoreType.DMA((4,)),
            pltpu.SemaphoreType.DMA((3,)),
            pltpu.SemaphoreType.DMA((9,)),
            pltpu.SemaphoreType.DMA((9,)),
            pltpu.SemaphoreType.REGULAR,
        ],
        compiler_params=pltpu.CompilerParams(
            collective_id=0, has_side_effects=True, vmem_limit_bytes=24 * 2**20),
    )(*[pltpu.with_memory_space_constraint(x, pltpu.HBM)
        for x in (velocity, diffusion, wall_types, stretch_index)], bulk_target)
    return pl.pallas_call(
        finish_kernel,
        name="finish",
        out_shape=jax.ShapeDtypeStruct((3, CELLS) + plane, F32),
        in_specs=[vmem] * 3,
        out_specs=hbm,
        scratch_shapes=[pltpu.VMEM((CELLS,) + plane, F32), pltpu.SemaphoreType.DMA((3, 4))],
        compiler_params=pltpu.CompilerParams(vmem_limit_bytes=24 * 2**20),
    )(*mids)


def solution(mesh):
    return jax.shard_map(
        shards,
        mesh=mesh,
        in_specs=(P(None, "gz", "gy", None), P("gy", None), P("gy", None), P(), P()),
        out_specs=P(None, "gz", "gy", None),
        check_vma=False,
    )
```
